768 devices in a mesh: seq: 24 (over z, core), ctx: 32 (over x, y).
Axes of the slice: x: 4, y: 8, z: 12, core: 2. Of those that a mesh axis runs over, the one named last changes fastest.
Arguments:
- tokens: bfloat16 [98304, 2048], P(('seq', 'ctx')), parts along dimension 0, may hold values from -14 to 14
- queries: bfloat16 [98304, 2048], P(('seq', 'ctx')), parts along dimension 0, may hold values from -10 to 10
- keys: bfloat16 [98304, 512], P(('seq', 'ctx')), parts along dimension 0, may hold values from -10 to 10
- values: bfloat16 [98304, 512], P(('seq', 'ctx')), parts along dimension 0, may hold values from -6 to 6
- norm_gain: bfloat16 [2048], replicated, may hold values from 0.5 to 1.5
- router: bfloat16 [2048, 32], replicated, may hold values from -0.375 to 0.375
- w_gate: bfloat16 [32, 2048, 512], P('ctx'), may hold values from -0.125 to 0.125
- w_up: bfloat16 [32, 2048, 512], P('ctx'), may hold values from -0.125 to 0.125
- w_down: bfloat16 [32, 512, 2048], P('ctx'), may hold values from -0.25 to 0.25
- picks: int32 [98304, 2], P(('seq', 'ctx')), parts along dimension 0, may hold values from 0 to 31, all different within a row
Outputs:
- layer: bfloat16 [98304, 2048], P(('seq', 'ctx')), parts along dimension 0
The draws below stay inside these ranges and needn't reach their ends.
There are 24 independent parts, one for each index of `seq`. The reference program is written for one: setup_inputs(seed, part) draws one part's arguments, and reference() takes and returns one part's arrays. A program takes and returns all parts, laid end to end along the dimension named above; an argument that names none is the same for every part. Nothing has to cross between parts.
All inputs are finite; a program needn't handle non-finite values.
Results may differ from the reference program's by a relative error of at most 0.0054.
Values may be sent and summed in bfloat16 or wider, within the bound.
A program may use at most 64 MiB of HBM per device.

```python
import math
import jax
import jax.numpy as jnp
from jax import lax

D = 2048
HEADS = 16
KV_HEADS = 4
HEAD_DIM = 128
FF_WIN = 512
TOPK = 2
ITERS = 8
TOK_DEV = 128
TOKENS = 4096
EXPERTS = 32
CAP = 8
N_CTX = 32


def draw_tokens(key, part):
    key_base = jax.random.fold_in(key, 11)
    key_first = jax.random.fold_in(key, 12)
    key_second = jax.random.fold_in(key, 13)
    phase = math.pi * jnp.arange(TOKENS, dtype=jnp.float32) / TOKENS
    first_dir = jax.random.normal(key_first, (D,), jnp.float32)
    second_dir = jax.random.normal(key_second, (D,), jnp.float32)
    base = jax.random.normal(key_base, (TOKENS, D), jnp.float32)
    amplitude = 1.5
    drift = jnp.cos(phase)[:, None] * first_dir[None, :] + jnp.sin(phase)[:, None] * second_dir[None, :]
    return jnp.clip(base + amplitude * drift, -14.0, 14.0).astype(jnp.bfloat16)


def block_levels(stream_key, dims, pieces, low, top_value):
    def one(dim, parts):
        steps = jax.random.uniform(jax.random.fold_in(jax.random.fold_in(stream_key, 6), dim), (parts,), jnp.float32, low / len(pieces), top_value / len(pieces))
        return jnp.repeat(jnp.exp(steps), dims[dim] // parts).reshape((-1,) + (1,) * (len(dims) - dim - 1))

    level = one(*pieces[0])
    for cut in pieces[1:]:
        level = level * one(*cut)
    return level


def distinct(stream_key, rows, amount, top, lift):
    order = jax.random.permutation(jax.random.fold_in(stream_key, 1), amount)
    boost = order
    for power in range(3):
        boost = boost * boost // amount
    boost = boost * lift // amount
    chance = jax.random.randint(jax.random.fold_in(stream_key, 2), (rows, amount), 0, 4096) + boost
    fixed_rows = jax.random.permutation(jax.random.fold_in(stream_key, 3), rows)[jnp.arange(amount) % rows]
    chance = jnp.where(jnp.arange(rows)[:, None] == fixed_rows[None, :], 1 << 14, chance)
    priority = chance * amount + jnp.arange(amount)
    return lax.top_k(priority.astype(jnp.int32), top)[1].astype(jnp.int32)


def centred(key, extent, scale, reach, cuts=(), kind=jnp.bfloat16):
    factor_of = block_levels(key, extent, cuts, -0.22, 0.18) if cuts else 1.0
    drawn = jax.random.normal(key, extent, jnp.float32) * scale * factor_of
    return jnp.minimum(jnp.maximum(drawn, -reach), reach).astype(kind)


def setup_inputs(seed: int = 0, part: int = 0) -> dict:
    streams_of = jax.random.split(jax.random.key(seed), 11)
    part_keys = jax.random.split(jax.random.fold_in(streams_of[10], part), 11)
    tokens = draw_tokens(jax.random.fold_in(jax.random.fold_in(streams_of[10], part), 71), part)
    queries = centred(part_keys[1], (TOKENS, HEADS * HEAD_DIM), 1.7, 10.0, ((0, 32),))
    keys = centred(part_keys[2], (TOKENS, KV_HEADS * HEAD_DIM), 1.7, 10.0, ((0, 32),))
    values = centred(part_keys[3], (TOKENS, KV_HEADS * HEAD_DIM), 1.0, 6.0, ((0, 32),))
    norm_gain = jnp.clip(1.0 + 0.1 * jax.random.normal(streams_of[4], (D,), jnp.float32), 0.5, 1.5).astype(jnp.bfloat16)
    router = centred(streams_of[5], (D, EXPERTS), (D // 9) ** -0.5, 0.375)
    w_gate = centred(streams_of[6], (EXPERTS, D, FF_WIN), D ** -0.5, 0.125, ((0, 32),))
    w_up = centred(streams_of[7], (EXPERTS, D, FF_WIN), D ** -0.5, 0.125, ((0, 32),))
    w_down = centred(streams_of[8], (EXPERTS, FF_WIN, D), FF_WIN ** -0.5, 0.25, ((0, 32),))
    picks = distinct(part_keys[9], TOKENS, EXPERTS, TOPK, 512)
    return dict(tokens=tokens, queries=queries, keys=keys, values=values, norm_gain=norm_gain, router=router, w_gate=w_gate, w_up=w_up, w_down=w_down, picks=picks)


score_cap = 50.0
logit_cap = 10.0
epsilon = 1e-06

def attend(queries, keys, values):
    group = HEADS // KV_HEADS
    query_heads = queries.astype(jnp.float32).reshape(TOKENS, KV_HEADS, group, HEAD_DIM)
    key_heads = keys.astype(jnp.float32).reshape(TOKENS, KV_HEADS, HEAD_DIM)
    value_heads = values.astype(jnp.float32).reshape(TOKENS, KV_HEADS, HEAD_DIM)
    block_size = math.gcd(TOKENS, 512)
    results = []
    for first_row in range(0, TOKENS, block_size):
        last_row = first_row + block_size
        scores = jnp.einsum('tkgd,rkd->kgtr', query_heads[first_row:last_row], key_heads[:last_row], precision=lax.Precision.HIGHEST) / math.sqrt(HEAD_DIM)
        weights = jnp.exp(score_cap * jnp.tanh(scores / score_cap))
        visible = jnp.arange(last_row, dtype=jnp.int32)[None, :] <= (first_row + jnp.arange(block_size, dtype=jnp.int32))[:, None]
        weights = jnp.where(visible[None, None], weights, jnp.float32(0.0))
        denom = lax.optimization_barrier(jnp.sum(weights, -1))
        rounded = lax.optimization_barrier(weights.astype(jnp.bfloat16)).astype(jnp.float32)
        summed = jnp.einsum('kgtr,rkd->tkgd', rounded, value_heads[:last_row], precision=lax.Precision.HIGHEST)
        results.append((summed / jnp.transpose(denom, (2, 0, 1))[..., None]).reshape(block_size, -1).astype(jnp.bfloat16))
    return jnp.concatenate(results, 0)

def run_expert(operands):
    inputs, gate_weight, up_weight, down_weight = operands
    gate = jnp.dot(inputs, gate_weight, preferred_element_type=jnp.float32)
    upward = jnp.dot(inputs, up_weight, preferred_element_type=jnp.float32)
    hidden = (jax.nn.silu(gate) * upward).astype(jnp.bfloat16)
    return jnp.dot(hidden, down_weight, preferred_element_type=jnp.float32).astype(jnp.bfloat16)

def reference(tokens, queries, keys, values, norm_gain, router, w_gate, w_up, w_down, picks):
    attended = attend(queries, keys, values)
    stream = (tokens.astype(jnp.float32) + attended.astype(jnp.float32)).astype(jnp.bfloat16).astype(jnp.float32)
    mean_square = lax.optimization_barrier(jnp.mean(stream * stream, -1, keepdims=True))
    normed = (stream * lax.rsqrt(mean_square + epsilon) * norm_gain.astype(jnp.float32)).astype(jnp.bfloat16)
    logits = logit_cap * jnp.tanh(jnp.dot(normed, router, preferred_element_type=jnp.float32) / logit_cap)
    plan = jnp.exp(logits)
    plan = plan / lax.optimization_barrier(jnp.sum(plan, -1, keepdims=True))
    target = TOKENS * TOPK / EXPERTS
    for sweep in range(ITERS):
        columns = lax.optimization_barrier(jnp.sum(plan, 0))
        plan = plan * (target / columns)
        plan = plan * (TOPK / lax.optimization_barrier(jnp.sum(plan, -1, keepdims=True)))
    chosen = jnp.take_along_axis(plan, picks, 1)
    gates = chosen / lax.optimization_barrier(jnp.sum(chosen, -1, keepdims=True))
    flags = (picks[:, :, None] == jnp.arange(EXPERTS, dtype=jnp.int32)[None, None, :]).astype(jnp.int32)
    flags = flags.reshape(N_CTX, TOK_DEV * TOPK, EXPERTS)
    ranks = jnp.cumsum(flags, 1) - flags
    slots = lax.optimization_barrier(jnp.sum(ranks * flags, -1)).reshape(TOKENS, TOPK).astype(jnp.int32)
    kept = slots < CAP
    source = jnp.broadcast_to((jnp.arange(TOKENS, dtype=jnp.int32) // TOK_DEV)[:, None], (TOKENS, TOPK))
    flat_index = jnp.where(kept, picks * CAP + slots, EXPERTS * CAP).astype(jnp.int32)
    buffer = jnp.zeros((N_CTX, EXPERTS * CAP + 1, D), normed.dtype)
    buffer = buffer.at[source, flat_index].set(jnp.broadcast_to(normed[:, None, :], (TOKENS, TOPK, D)))
    inputs = buffer[:, :EXPERTS * CAP].reshape(N_CTX, EXPERTS, CAP, D).transpose(1, 0, 2, 3).reshape(EXPERTS, N_CTX * CAP, D)
    outputs = lax.map(run_expert, (inputs, w_gate, w_up, w_down)).reshape(EXPERTS, N_CTX, CAP, D)
    gathered = outputs[picks, source, jnp.minimum(slots, CAP - 1)]
    scale = jnp.where(kept, gates, jnp.float32(0.0))
    mixture = lax.optimization_barrier(jnp.sum(gathered.astype(jnp.float32) * scale[:, :, None], 1))
    return (stream + mixture).astype(jnp.bfloat16)
```

```python
import math

import jax
import jax.numpy as jnp
from jax import lax
from jax.experimental import pallas as pl
from jax.experimental.pallas import tpu as pltpu
from jax.sharding import PartitionSpec as P

HEADS = 16
KV_HEADS = 4
HEAD_DIM = 128
ITERS = 8


score_cap = 50.0
logit_cap = 10.0
epsilon = 1e-06


def key_block_loop(query_heads, positions, latest, key_rows, value_rows, block_size):

    def advance(block_index, running):
        key_first = block_index * block_size

        def compute(current):
            summed, denom = current
            key_block = lax.dynamic_slice_in_dim(key_rows, key_first, block_size, 0)
            value_block = lax.dynamic_slice_in_dim(value_rows, key_first, block_size, 0)
            scores = jnp.einsum(
                "tkgd,rkd->kgtr", query_heads, key_block, preferred_element_type=jnp.float32
            ) / math.sqrt(HEAD_DIM)
            weights = jnp.exp(score_cap * jnp.tanh(scores / score_cap))
            key_positions = key_first + jnp.arange(block_size, dtype=jnp.int32)
            visible = key_positions[None, None, None, :] <= positions[None, None, :, None]
            weights = jnp.where(visible, weights, 0.0)
            denom = denom + jnp.sum(weights, -1)
            summed = summed + jnp.einsum(
                "kgtr,rkd->tkgd",
                weights.astype(jnp.bfloat16),
                value_block,
                preferred_element_type=jnp.float32,
            )
            return (summed, denom)

        def unchanged(current):
            return current

        return lax.cond(key_first <= latest, compute, unchanged, running)

    return advance


def attend(query_sets, keys, values):
    group = HEADS // KV_HEADS
    prepared = []
    initial = []
    for query_rows, positions in query_sets:
        length = query_rows.shape[0]
        prepared.append(
            (query_rows.reshape(length, KV_HEADS, group, HEAD_DIM), positions, jnp.max(positions))
        )
        initial.append(
            (
                jnp.zeros((length, KV_HEADS, group, HEAD_DIM), jnp.float32),
                jnp.zeros((KV_HEADS, group, length), jnp.float32),
            )
        )
    running = tuple(initial)
    key_piece = lax.all_gather(keys, "ctx", axis=0, tiled=True)
    value_piece = lax.all_gather(values, "ctx", axis=0, tiled=True)
    piece_rows = key_piece.shape[0]
    block_size = math.gcd(piece_rows, 512)
    key_rows = key_piece.reshape(piece_rows, KV_HEADS, HEAD_DIM)
    value_rows = value_piece.reshape(piece_rows, KV_HEADS, HEAD_DIM)
    updated = []
    for (query_heads, positions, latest), current in zip(prepared, running):
        advance = key_block_loop(query_heads, positions, latest, key_rows, value_rows, block_size)
        updated.append(lax.fori_loop(0, piece_rows // block_size, advance, current))
    finished = tuple(updated)
    results = []
    for summed, denom in finished:
        normal_out = summed / jnp.transpose(denom, (2, 0, 1))[..., None]
        results.append(normal_out.reshape(summed.shape[0], -1).astype(jnp.bfloat16))
    return results


MESH = pl.DeviceIdType.MESH
NX = 4
NY = 8
PEERS = NX * NY
SLOTS = 8
VMEM_LIMIT = 56 * 1024 * 1024


def shifted(me, dx, dy):
    return lax.rem(me // NY + dx + NX, NX) * NY + lax.rem(lax.rem(me, NY) + dy + NY, NY)


def moe_kernel(
    tokens,
    attended,
    gain,
    router,
    picks,
    w_gate,
    w_up,
    w_down,
    layer,
    gate_w,
    up_w,
    down_w,
    resid,
    outbox,
    inbox,
    results,
    returns,
    plans,
    weight_sem,
    plan_send,
    plan_recv,
    out_send,
    out_recv,
    back_send,
    back_recv,
):
    me = lax.axis_index("ctx")
    rows, width = tokens.shape
    experts = router.shape[1]

    def to_peer(k):
        return shifted(me, k // NY, lax.rem(k, NY))

    def from_peer(k):
        return shifted(me, -(k // NY), -lax.rem(k, NY))

    barrier = pltpu.get_barrier_semaphore()

    @pl.loop(1, PEERS)
    def _(k):
        pl.semaphore_signal(barrier, inc=1, device_id={"ctx": to_peer(k)}, device_id_type=MESH)

    loads = [
        pltpu.make_async_copy(src, dst, weight_sem.at[i])
        for i, (src, dst) in enumerate(((w_gate, gate_w), (w_up, up_w), (w_down, down_w)))
    ]
    for load in loads:
        load.start()

    stream = (tokens[...].astype(jnp.float32) + attended[...].astype(jnp.float32)).astype(
        jnp.bfloat16
    )
    resid[...] = stream
    stream = stream.astype(jnp.float32)
    mean_square = jnp.mean(stream * stream, -1, keepdims=True)
    normed = (stream * lax.rsqrt(mean_square + epsilon) * gain[...].astype(jnp.float32)).astype(
        jnp.bfloat16
    )
    logits = logit_cap * jnp.tanh(
        jnp.dot(normed, router[...], preferred_element_type=jnp.float32) / logit_cap
    )
    plan = jnp.exp(logits.T)
    plan = plan / jnp.sum(plan, 0, keepdims=True)
    plans[0] = plan.astype(jnp.bfloat16)

    pl.semaphore_wait(barrier, PEERS - 1)

    def plan_column(dy):
        return pltpu.make_async_remote_copy(
            src_ref=plans.at[0],
            dst_ref=plans.at[dy],
            send_sem=plan_send.at[dy],
            recv_sem=plan_recv.at[dy],
            device_id={"ctx": shifted(me, 0, dy)},
            device_id_type=MESH,
        )

    def plan_row(dx):
        return pltpu.make_async_remote_copy(
            src_ref=plans.at[pl.ds(0, NY)],
            dst_ref=plans.at[pl.ds(dx * NY, NY)],
            send_sem=plan_send.at[NY + dx],
            recv_sem=plan_recv.at[NY + dx],
            device_id={"ctx": shifted(me, dx, 0)},
            device_id_type=MESH,
        )

    for dy in range(1, NY):
        plan_column(dy).start()

    picked = picks[...]
    offset = lax.rem(picked // NY - me // NY + NX, NX) * NY + lax.rem(
        lax.rem(picked, NY) - lax.rem(me, NY) + NY, NY
    )
    number = lax.broadcasted_iota(jnp.int32, (PEERS, rows), 0)
    chosen = [number == offset[j : j + 1] for j in range(2)]
    either = jnp.where(chosen[0] | chosen[1], 1.0, 0.0)
    earlier = jnp.where(
        lax.broadcasted_iota(jnp.int32, (rows, rows), 0)
        < lax.broadcasted_iota(jnp.int32, (rows, rows), 1),
        1.0,
        0.0,
    ).astype(jnp.bfloat16)
    ranks = jnp.dot(either.astype(jnp.bfloat16), earlier, preferred_element_type=jnp.float32)
    place = jnp.where(either > 0.0, ranks, -1.0)
    slot = lax.broadcasted_iota(jnp.int32, (PEERS, SLOTS, rows), 1).astype(jnp.float32)
    held = jnp.where(place[:, None, :] == slot, 1.0, 0.0).reshape(PEERS * SLOTS, rows)
    packed = jnp.dot(held.astype(jnp.bfloat16), normed, preferred_element_type=jnp.float32)
    packed = packed.astype(jnp.bfloat16).reshape(PEERS, SLOTS, width)
    outbox[...] = packed

    def outward(k):
        return pltpu.make_async_remote_copy(
            src_ref=outbox.at[k],
            dst_ref=inbox.at[k],
            send_sem=out_send.at[k],
            recv_sem=out_recv.at[k],
            device_id={"ctx": to_peer(k)},
            device_id_type=MESH,
        )

    def backward(k):
        return pltpu.make_async_remote_copy(
            src_ref=results.at[k],
            dst_ref=returns.at[k],
            send_sem=back_send.at[k],
            recv_sem=back_recv.at[k],
            device_id={"ctx": from_peer(k)},
            device_id_type=MESH,
        )

    @pl.loop(1, PEERS)
    def _(k):
        outward(k).start()

    inbox[0] = outbox[0]

    for dy in range(1, NY):
        plan_column(dy).wait_recv()
    for dx in range(1, NX):
        plan_row(dx).start()

    for load in loads:
        load.wait()

    @pl.loop(0, NX)
    def _(chunk):
        first = chunk * NY

        @pl.loop(jnp.maximum(first, 1), first + NY)
        def _(k):
            outward(k).wait_recv()

        block = inbox[pl.ds(first, NY)].reshape(NY * SLOTS, width)
        gate = jnp.dot(block, gate_w[...], preferred_element_type=jnp.float32)
        upward = jnp.dot(block, up_w[...], preferred_element_type=jnp.float32)
        hidden = (gate / (1.0 + jnp.exp(-gate)) * upward).astype(jnp.bfloat16)
        given = jnp.dot(hidden, down_w[...], preferred_element_type=jnp.float32)
        results[pl.ds(first, NY)] = given.astype(jnp.bfloat16).reshape(NY, SLOTS, width)

        @pl.loop(jnp.maximum(first, 1), first + NY)
        def _(k):
            backward(k).start()

    returns[0] = results[0]

    for dx in range(1, NX):
        plan_row(dx).wait_recv()

    target = float(rows * PEERS * 2 / experts)

    def column_sums(scale):
        def add(s, total):
            block = plans[s].astype(jnp.float32)
            if scale is None:
                return total + block
            return total + block * (2.0 / jnp.sum(block * scale, 0, keepdims=True))

        total = lax.fori_loop(0, PEERS, add, jnp.zeros((experts, rows), jnp.float32), unroll=4)
        return jnp.sum(total, 1, keepdims=True)

    scale = target / column_sums(None)
    scale = lax.fori_loop(0, ITERS - 1, lambda _, s: target / column_sums(s), scale)
    plan = plan * scale
    plan = plan * (2.0 / jnp.sum(plan, 0, keepdims=True))
    named = lax.broadcasted_iota(jnp.int32, (experts, rows), 0)
    mass = [
        jnp.sum(jnp.where(named == picked[j : j + 1], plan, 0.0), 0, keepdims=True)
        for j in range(2)
    ]
    total = mass[0] + mass[1]
    gates = jnp.where(chosen[0], mass[0] / total, 0.0) + jnp.where(chosen[1], mass[1] / total, 0.0)
    mixing = jnp.where(place[:, None, :] == slot, gates[:, None, :], 0.0)
    mixing = mixing.reshape(PEERS * SLOTS, rows).T
    high = mixing.astype(jnp.bfloat16)
    low = (mixing - high.astype(jnp.float32)).astype(jnp.bfloat16)

    @pl.loop(1, PEERS)
    def _(k):
        backward(k).wait_recv()

    step = 512
    for first in range(0, width, step):
        columns = pl.ds(first, step)
        block = returns[:, :, columns].reshape(PEERS * SLOTS, step)
        mixture = jnp.dot(high, block, preferred_element_type=jnp.float32) + jnp.dot(
            low, block, preferred_element_type=jnp.float32
        )
        layer[:, columns] = (resid[:, columns].astype(jnp.float32) + mixture).astype(jnp.bfloat16)

    @pl.loop(1, PEERS)
    def _(k):
        outward(k).wait_send()
        backward(k).wait_send()

    for dy in range(1, NY):
        plan_column(dy).wait_send()
    for dx in range(1, NX):
        plan_row(dx).wait_send()


def experts_of(tokens, attended, norm_gain, router, w_gate, w_up, w_down, picks):
    rows, width = tokens.shape
    hidden = w_gate.shape[-1]
    experts = router.shape[1]
    whole = pl.BlockSpec(memory_space=pltpu.VMEM)
    apart = pl.BlockSpec(memory_space=pl.ANY)
    box = pltpu.VMEM((PEERS, SLOTS, width), jnp.bfloat16)
    sems = pltpu.SemaphoreType.DMA
    return pl.pallas_call(
        moe_kernel,
        out_shape=jax.ShapeDtypeStruct((rows, width), jnp.bfloat16),
        in_specs=[whole] * 5 + [apart] * 3,
        out_specs=whole,
        scratch_shapes=[
            pltpu.VMEM((width, hidden), jnp.bfloat16),
            pltpu.VMEM((width, hidden), jnp.bfloat16),
            pltpu.VMEM((hidden, width), jnp.bfloat16),
            pltpu.VMEM((rows, width), jnp.bfloat16),
            box,
            box,
            box,
            box,
            pltpu.VMEM((PEERS, experts, rows), jnp.bfloat16),
            sems((3,)),
            sems((NY + NX,)),
            sems((NY + NX,)),
            sems((PEERS,)),
            sems((PEERS,)),
            sems((PEERS,)),
            sems((PEERS,)),
        ],
        compiler_params=pltpu.CompilerParams(
            collective_id=1, has_side_effects=True, vmem_limit_bytes=VMEM_LIMIT
        ),
        name="experts",
    )(
        tokens,
        attended,
        norm_gain.reshape(1, width),
        router,
        picks.T,
        w_gate[0],
        w_up[0],
        w_down[0],
    )


def per_device(tokens, queries, keys, values, norm_gain, router, w_gate, w_up, w_down, picks):
    my_index = lax.axis_index("ctx")
    my_rows = tokens.shape[0]
    offsets = jnp.arange(my_rows, dtype=jnp.int32) + my_index * my_rows
    attended = attend([(queries, offsets)], keys, values)[0]
    return experts_of(tokens, attended, norm_gain, router, w_gate, w_up, w_down, picks)


def solution(mesh):
    placed = (
        P(("seq", "ctx"), None),
        P(("seq", "ctx"), None),
        P(("seq", "ctx"), None),
        P(("seq", "ctx"), None),
        P(),
        P(),
        P("ctx", None, None),
        P("ctx", None, None),
        P("ctx", None, None),
        P(("seq", "ctx"), None),
    )
    return jax.shard_map(
        per_device, mesh=mesh, in_specs=placed, out_specs=P(("seq", "ctx"), None), check_vma=False
    )
```

```python
import math

import jax
import jax.numpy as jnp
from jax import lax
from jax.experimental import pallas as pl
from jax.experimental.pallas import tpu as pltpu
from jax.sharding import PartitionSpec as P

HEADS = 16
KV_HEADS = 4
GROUP = HEADS // KV_HEADS
HEAD_DIM = 128
ITERS = 8
MESH = pl.DeviceIdType.MESH
NX = 4
NY = 8
PEERS = NX * NY
SLOTS = 8
VMEM_LIMIT = 48 * 1024 * 1024


score_cap = 50.0
logit_cap = 10.0
epsilon = 1e-06


def shifted(me, dx, dy):
    return lax.rem(me // NY + dx + NX, NX) * NY + lax.rem(lax.rem(me, NY) + dy + NY, NY)


def contract_last(left, right):
    return lax.dot_general(
        left, right, (((1,), (1,)), ((), ())), preferred_element_type=jnp.float32
    )


def layer_kernel(
    tokens,
    gain,
    router,
    picks,
    queries,
    keys,
    values,
    w_gate,
    w_up,
    w_down,
    layer,
    gate_w,
    up_w,
    down_w,
    query_rows,
    pairs,
    summed,
    denoms,
    finished,
    attended,
    resid,
    held,
    outbox,
    inbox,
    results,
    returns,
    plans,
    weight_sem,
    own_sem,
    head_send,
    head_recv,
    ring_send,
    ring_recv,
    done_send,
    done_recv,
    plan_send,
    plan_recv,
    out_send,
    out_recv,
    back_send,
    back_recv,
):
    me = lax.axis_index("ctx")
    my_x = me // NY
    my_y = lax.rem(me, NY)
    rows, width = tokens.shape
    experts = router.shape[0]
    group_width = GROUP * HEAD_DIM

    def to_peer(k):
        return shifted(me, k // NY, lax.rem(k, NY))

    def from_peer(k):
        return shifted(me, -(k // NY), -lax.rem(k, NY))

    barrier = pltpu.get_barrier_semaphore()

    @pl.loop(1, PEERS)
    def _(k):
        pl.semaphore_signal(barrier, inc=1, device_id={"ctx": to_peer(k)}, device_id_type=MESH)

    def head_columns(head):
        return pl.ds(pl.multiple_of(head * HEAD_DIM, HEAD_DIM), HEAD_DIM)

    def group_columns(head):
        return pl.ds(pl.multiple_of(head * group_width, group_width), group_width)

    own = [
        (keys.at[:, head_columns(my_x)], pairs.at[my_x, 0, 0]),
        (values.at[:, head_columns(my_x)], pairs.at[my_x, 0, 1]),
        (queries.at[:, group_columns(my_x)], query_rows.at[my_x]),
    ]
    own = [pltpu.make_async_copy(src, dst, own_sem.at[i]) for i, (src, dst) in enumerate(own)]
    for copy in own:
        copy.start()
    loads = [
        pltpu.make_async_copy(src, dst, weight_sem.at[i])
        for i, (src, dst) in enumerate(((w_gate, gate_w), (w_up, up_w), (w_down, down_w)))
    ]
    for load in loads:
        load.start()

    def to_head(dx, part):
        head = lax.rem(my_x + dx, NX)
        if part == 2:
            src, dst = queries.at[:, group_columns(head)], query_rows.at[my_x]
        else:
            src = (keys, values)[part].at[:, head_columns(head)]
            dst = pairs.at[my_x, 0, part]
        return pltpu.make_async_remote_copy(
            src_ref=src,
            dst_ref=dst,
            send_sem=head_send.at[dx, part],
            recv_sem=head_recv.at[dx, part],
            device_id={"ctx": shifted(me, dx, 0)},
            device_id_type=MESH,
        )

    def from_head(dx, part):
        source = lax.rem(my_x - dx + NX, NX)
        dst = query_rows.at[source] if part == 2 else pairs.at[source, 0, part]
        return pltpu.make_async_remote_copy(
            src_ref=dst,
            dst_ref=dst,
            send_sem=head_send.at[dx, part],
            recv_sem=head_recv.at[dx, part],
            device_id={"ctx": shifted(me, dx, 0)},
            device_id_type=MESH,
        )

    pl.semaphore_wait(barrier, PEERS - 1)
    for part in range(3):
        for dx in range(1, NX):
            to_head(dx, part).start()

    picked = picks[...]
    offset = lax.rem(picked // NY - my_x + NX, NX) * NY + lax.rem(
        lax.rem(picked, NY) - my_y + NY, NY
    )
    number = lax.broadcasted_iota(jnp.int32, (PEERS, rows), 0)
    chosen = [number == offset[j : j + 1] for j in range(2)]
    either = jnp.where(chosen[0] | chosen[1], 1.0, 0.0)
    earlier = jnp.where(
        lax.broadcasted_iota(jnp.int32, (rows, rows), 0)
        < lax.broadcasted_iota(jnp.int32, (rows, rows), 1),
        1.0,
        0.0,
    ).astype(jnp.bfloat16)
    ranks = jnp.dot(either.astype(jnp.bfloat16), earlier, preferred_element_type=jnp.float32)
    place = jnp.where(either > 0.0, ranks, -1.0)
    slot = lax.broadcasted_iota(jnp.int32, (PEERS, SLOTS, rows), 1).astype(jnp.float32)
    rows_held = jnp.where(place[:, None, :] == slot, 1.0, 0.0).reshape(PEERS * SLOTS, rows)
    held[...] = rows_held.astype(jnp.bfloat16)

    summed[...] = jnp.zeros_like(summed)
    denoms[...] = jnp.zeros_like(denoms)

    def behind(step):
        return lax.select(step == 0, 0, 2 * step - 1)

    def ahead(step):
        return lax.select(step == 4, 7, 2 * step)

    def ring(up, step, i):
        block = lax.rem(my_x - i + NX, NX)
        place_of = behind if up else ahead
        way = 0 if up else 1
        return pltpu.make_async_remote_copy(
            src_ref=pairs.at[block, place_of(step - 1)],
            dst_ref=pairs.at[block, place_of(step)],
            send_sem=ring_send.at[way, step, i],
            recv_sem=ring_recv.at[way, step, i],
            device_id={"ctx": shifted(me, 0, 1 if up else -1)},
            device_id_type=MESH,
        )

    def forward(step, i):
        step = jnp.int32(step)

        @pl.when((step < 3) | (i < 2))
        def _():
            ring(True, step + 1, i).start()

        @pl.when((step < 3) | (i >= 2))
        def _():
            ring(False, step + 1, i).start()

    def attend(q_block, key_block, value_block, diagonal=False):
        block = query_rows[q_block]
        query = jnp.concatenate(
            [block[:, h * HEAD_DIM : (h + 1) * HEAD_DIM] for h in range(GROUP)], 0
        )
        scores = contract_last(query, key_block)
        weights = jnp.exp2(
            jnp.tanh(scores * (1.0 / (score_cap * math.sqrt(HEAD_DIM))))
            * (score_cap * math.log2(math.e))
        )
        if diagonal:
            row = lax.broadcasted_iota(jnp.int32, (GROUP, rows, rows), 1)
            column = lax.broadcasted_iota(jnp.int32, (GROUP, rows, rows), 2)
            visible = (column <= row).reshape(GROUP * rows, rows)
            weights = jnp.where(visible, weights, 0.0)
        part = weights[:, :rows]
        for first in range(rows, weights.shape[1], rows):
            part = part + weights[:, first : first + rows]
        denoms[q_block] += part
        summed[q_block] += jnp.dot(
            weights.astype(jnp.bfloat16), value_block, preferred_element_type=jnp.float32
        )

    def unit(block, where):
        return pairs[block, where, 0], pairs[block, where, 1]

    def attend_own(i):
        block = lax.rem(my_x - i + NX, NX)
        own_keys, own_values = unit(block, 0)
        attend(block, own_keys, own_values, diagonal=True)

        @pl.loop(block + 1, NX)
        def _(q_block):
            attend(q_block, own_keys, own_values)

    def attend_two(step, i):
        block = lax.rem(my_x - i + NX, NX)

        @pl.when(my_y >= step)
        def _():
            attend(block, *unit(block, 2 * step - 1))

        @pl.when(my_y >= NY - step)
        def _():
            attend(block, *unit(block, 2 * step))

        @pl.loop(block + 1, NX)
        def _(q_block):
            first, second = unit(block, 2 * step - 1), unit(block, 2 * step)
            attend(
                q_block,
                jnp.concatenate([first[0], second[0]], 0),
                jnp.concatenate([first[1], second[1]], 0),
            )

    def attend_opposite(i):
        block = lax.rem(my_x - i + NX, NX)

        @pl.when(my_y >= NY // 2)
        def _():
            attend(block, *unit(block, 7))

        @pl.loop(block + 1, NX)
        def _(q_block):
            attend(q_block, *unit(block, 7))

    for copy in own[:2]:
        copy.wait()
    forward(0, 0)
    for dx in range(1, NX):
        from_head(dx, 0).wait_recv()
        from_head(dx, 1).wait_recv()
        forward(0, dx)
    own[2].wait()
    for dx in range(1, NX):
        from_head(dx, 2).wait_recv()

    def arrive(step, i):
        ring(True, step, i).wait_recv()
        ring(False, step, i).wait_recv()
        forward(step, i)

    @pl.loop(0, NX)
    def _(i):
        arrive(jnp.int32(1), i)
        attend_own(i)

    @pl.loop(2, 4)
    def _(step):
        @pl.loop(0, NX)
        def _(i):
            arrive(step, i)
            attend_two(step - 1, i)

    @pl.loop(0, NX)
    def _(i):
        attend_two(3, i)

        @pl.when(i < 2)
        def _():
            ring(True, jnp.int32(4), i).wait_recv()

        @pl.when(i >= 2)
        def _():
            ring(False, jnp.int32(4), i).wait_recv()

        attend_opposite(i)

    def give(dx):
        block = lax.rem(my_x + dx, NX)
        return pltpu.make_async_remote_copy(
            src_ref=finished.at[block],
            dst_ref=attended.at[my_x],
            send_sem=done_send.at[dx],
            recv_sem=done_recv.at[dx],
            device_id={"ctx": shifted(me, dx, 0)},
            device_id_type=MESH,
        )

    def take(dx):
        source = lax.rem(my_x - dx + NX, NX)
        return pltpu.make_async_remote_copy(
            src_ref=attended.at[source],
            dst_ref=attended.at[source],
            send_sem=done_send.at[dx],
            recv_sem=done_recv.at[dx],
            device_id={"ctx": shifted(me, dx, 0)},
            device_id_type=MESH,
        )

    def normal(block):
        denom = jnp.sum(denoms[block], -1, keepdims=True)
        return (summed[block] / denom).astype(jnp.bfloat16).reshape(GROUP, rows, HEAD_DIM)

    @pl.loop(1, NX)
    def _(dx):
        block = lax.rem(my_x + dx, NX)
        finished[block] = normal(block)
        give(dx).start()

    attended[my_x] = normal(my_x)

    @pl.loop(1, NX)
    def _(dx):
        take(dx).wait_recv()

    square = jnp.zeros((rows, HEAD_DIM), jnp.float32)
    for h in range(HEADS):
        columns = slice(h * HEAD_DIM, (h + 1) * HEAD_DIM)
        stream = (
            tokens[:, columns].astype(jnp.float32)
            + attended[h // GROUP, h % GROUP].astype(jnp.float32)
        ).astype(jnp.bfloat16)
        resid[:, columns] = stream
        stream = stream.astype(jnp.float32)
        square = square + stream * stream
    mean_square = jnp.sum(square, -1, keepdims=True) / width
    normed = (
        resid[...].astype(jnp.float32)
        * lax.rsqrt(mean_square + epsilon)
        * gain[...].astype(jnp.float32)
    ).astype(jnp.bfloat16)

    def outward(k):
        return pltpu.make_async_remote_copy(
            src_ref=outbox.at[k],
            dst_ref=inbox.at[k],
            send_sem=out_send.at[k],
            recv_sem=out_recv.at[k],
            device_id={"ctx": to_peer(k)},
            device_id_type=MESH,
        )

    def backward(k):
        return pltpu.make_async_remote_copy(
            src_ref=results.at[k],
            dst_ref=returns.at[k],
            send_sem=back_send.at[k],
            recv_sem=back_recv.at[k],
            device_id={"ctx": from_peer(k)},
            device_id_type=MESH,
        )

    for chunk in range(NX):
        first = chunk * NY
        packed = jnp.dot(
            held[first * SLOTS : (first + NY) * SLOTS], normed, preferred_element_type=jnp.float32
        )
        packed = packed.astype(jnp.bfloat16).reshape(NY, SLOTS, width)
        outbox[first : first + NY] = packed
        if chunk == 0:
            inbox[0] = packed[0]

        @pl.loop(max(first, 1), first + NY)
        def _(k):
            outward(k).start()

    logits = logit_cap * jnp.tanh(contract_last(router[...], normed) / logit_cap)
    plan = jnp.exp(logits)
    plan = plan / jnp.sum(plan, 0, keepdims=True)
    plans[0] = plan.astype(jnp.bfloat16)

    def plan_column(dy):
        return pltpu.make_async_remote_copy(
            src_ref=plans.at[0],
            dst_ref=plans.at[dy],
            send_sem=plan_send.at[dy],
            recv_sem=plan_recv.at[dy],
            device_id={"ctx": shifted(me, 0, dy)},
            device_id_type=MESH,
        )

    def plan_row(dx):
        return pltpu.make_async_remote_copy(
            src_ref=plans.at[pl.ds(0, NY)],
            dst_ref=plans.at[pl.ds(dx * NY, NY)],
            send_sem=plan_send.at[NY + dx],
            recv_sem=plan_recv.at[NY + dx],
            device_id={"ctx": shifted(me, dx, 0)},
            device_id_type=MESH,
        )

    for dy in range(1, NY):
        plan_column(dy).start()

    for load in loads:
        load.wait()

    @pl.loop(0, NX)
    def _(chunk):
        first = chunk * NY

        @pl.loop(jnp.maximum(first, 1), first + NY)
        def _(k):
            outward(k).wait_recv()

        block = inbox[pl.ds(first, NY)].reshape(NY * SLOTS, width)
        gate = jnp.dot(block, gate_w[...], preferred_element_type=jnp.float32)
        upward = jnp.dot(block, up_w[...], preferred_element_type=jnp.float32)
        hidden = (gate / (1.0 + jnp.exp(-gate)) * upward).astype(jnp.bfloat16)
        given = jnp.dot(hidden, down_w[...], preferred_element_type=jnp.float32)
        results[pl.ds(first, NY)] = given.astype(jnp.bfloat16).reshape(NY, SLOTS, width)

        @pl.loop(jnp.maximum(first, 1), first + NY)
        def _(k):
            backward(k).start()

        @pl.when(chunk == 1)
        def _():
            for dy in range(1, NY):
                plan_column(dy).wait_recv()
            for dx in range(1, NX):
                plan_row(dx).start()

    returns[0] = results[0]

    for dx in range(1, NX):
        plan_row(dx).wait_recv()

    target = float(rows * PEERS * 2 / experts)

    def column_sums(scale):
        def add(s, total):
            block = plans[s].astype(jnp.float32)
            if scale is None:
                return total + block
            return total + block * (2.0 / jnp.sum(block * scale, 0, keepdims=True))

        total = lax.fori_loop(0, PEERS, add, jnp.zeros((experts, rows), jnp.float32), unroll=4)
        return jnp.sum(total, 1, keepdims=True)

    scale = target / column_sums(None)
    scale = lax.fori_loop(0, ITERS - 1, lambda _, s: target / column_sums(s), scale)
    plan = plan * scale
    plan = plan * (2.0 / jnp.sum(plan, 0, keepdims=True))
    named = lax.broadcasted_iota(jnp.int32, (experts, rows), 0)
    mass = [
        jnp.sum(jnp.where(named == picked[j : j + 1], plan, 0.0), 0, keepdims=True)
        for j in range(2)
    ]
    total = mass[0] + mass[1]
    gates = jnp.where(chosen[0], mass[0] / total, 0.0) + jnp.where(chosen[1], mass[1] / total, 0.0)
    mixing = jnp.where(place[:, None, :] == slot, gates[:, None, :], 0.0)
    mixing = mixing.reshape(PEERS * SLOTS, rows).T
    high = mixing.astype(jnp.bfloat16)
    low = (mixing - high.astype(jnp.float32)).astype(jnp.bfloat16)

    @pl.loop(1, PEERS)
    def _(k):
        backward(k).wait_recv()

    step = 512
    for first in range(0, width, step):
        columns = pl.ds(first, step)
        block = returns[:, :, columns].reshape(PEERS * SLOTS, step)
        mixture = jnp.dot(high, block, preferred_element_type=jnp.float32) + jnp.dot(
            low, block, preferred_element_type=jnp.float32
        )
        layer[:, columns] = (resid[:, columns].astype(jnp.float32) + mixture).astype(jnp.bfloat16)

    for part in range(3):
        for dx in range(1, NX):
            to_head(dx, part).wait_send()

    @pl.loop(1, 4)
    def _(step):
        @pl.loop(0, NX)
        def _(i):
            ring(True, step, i).wait_send()
            ring(False, step, i).wait_send()

    @pl.loop(0, 2)
    def _(i):
        ring(True, jnp.int32(4), i).wait_send()
        ring(False, jnp.int32(4), i + 2).wait_send()

    @pl.loop(1, NX)
    def _(dx):
        give(dx).wait_send()

    @pl.loop(1, PEERS)
    def _(k):
        outward(k).wait_send()
        backward(k).wait_send()

    for dy in range(1, NY):
        plan_column(dy).wait_send()
    for dx in range(1, NX):
        plan_row(dx).wait_send()


def per_device(tokens, queries, keys, values, norm_gain, router, w_gate, w_up, w_down, picks):
    rows, width = tokens.shape
    hidden = w_gate.shape[-1]
    experts = router.shape[1]
    whole = pl.BlockSpec(memory_space=pltpu.VMEM)
    apart = pl.BlockSpec(memory_space=pl.ANY)
    box = pltpu.VMEM((PEERS, SLOTS, width), jnp.bfloat16)
    sems = pltpu.SemaphoreType.DMA
    heads_of_block = pltpu.VMEM((NX, GROUP, rows, HEAD_DIM), jnp.bfloat16)
    running = pltpu.VMEM((NX, GROUP * rows, HEAD_DIM), jnp.float32)
    return pl.pallas_call(
        layer_kernel,
        out_shape=jax.ShapeDtypeStruct((rows, width), jnp.bfloat16),
        in_specs=[whole] * 4 + [apart] * 6,
        out_specs=whole,
        scratch_shapes=[
            pltpu.VMEM((width, hidden), jnp.bfloat16),
            pltpu.VMEM((width, hidden), jnp.bfloat16),
            pltpu.VMEM((hidden, width), jnp.bfloat16),
            pltpu.VMEM((NX, rows, GROUP * HEAD_DIM), jnp.bfloat16),
            pltpu.VMEM((NX, NY, 2, rows, HEAD_DIM), jnp.bfloat16),
            running,
            running,
            heads_of_block,
            heads_of_block,
            pltpu.VMEM((rows, width), jnp.bfloat16),
            pltpu.VMEM((PEERS * SLOTS, rows), jnp.bfloat16),
            box,
            box,
            box,
            box,
            pltpu.VMEM((PEERS, experts, rows), jnp.bfloat16),
            sems((3,)),
            sems((3,)),
            sems((NX, 3)),
            sems((NX, 3)),
            sems((2, 5, NX)),
            sems((2, 5, NX)),
            sems((NX,)),
            sems((NX,)),
            sems((NY + NX,)),
            sems((NY + NX,)),
            sems((PEERS,)),
            sems((PEERS,)),
            sems((PEERS,)),
            sems((PEERS,)),
        ],
        compiler_params=pltpu.CompilerParams(
            collective_id=1, has_side_effects=True, vmem_limit_bytes=VMEM_LIMIT
        ),
        name="layer",
    )(
        tokens,
        norm_gain.reshape(1, width),
        router.T,
        picks.T,
        queries,
        keys,
        values,
        w_gate[0],
        w_up[0],
        w_down[0],
    )


def solution(mesh):
    placed = (
        P(("seq", "ctx"), None),
        P(("seq", "ctx"), None),
        P(("seq", "ctx"), None),
        P(("seq", "ctx"), None),
        P(),
        P(),
        P("ctx", None, None),
        P("ctx", None, None),
        P("ctx", None, None),
        P(("seq", "ctx"), None),
    )
    return jax.shard_map(
        per_device, mesh=mesh, in_specs=placed, out_specs=P(("seq", "ctx"), None), check_vma=False
    )
```

```python
import math

import jax
import jax.numpy as jnp
from jax import lax
from jax.experimental import pallas as pl
from jax.experimental.pallas import tpu as pltpu
from jax.sharding import PartitionSpec as P

HEADS = 16
KV_HEADS = 4
GROUP = HEADS // KV_HEADS
HEAD_DIM = 128
ITERS = 8
MESH = pl.DeviceIdType.MESH
NX = 4
NY = 8
PEERS = NX * NY
SLOTS = 8
HEADS_AT_ONCE = 4
VMEM_LIMIT = 60 * 1024 * 1024


score_cap = 50.0
logit_cap = 10.0
epsilon = 1e-06


def shifted(me, dx, dy):
    return lax.rem(me // NY + dx + NX, NX) * NY + lax.rem(lax.rem(me, NY) + dy + NY, NY)


def contract_last(left, right):
    return lax.dot_general(
        left, right, (((1,), (1,)), ((), ())), preferred_element_type=jnp.float32
    )


def layer_kernel(
    tokens_in,
    gain_in,
    router_in,
    picks_in,
    queries,
    keys,
    values,
    w_gate,
    w_up,
    w_down,
    layer,
    tokens,
    gain,
    router,
    picks,
    gate_w,
    up_w,
    down_w,
    query_rows,
    pairs,
    summed,
    denoms,
    finished,
    attended,
    resid,
    held,
    outbox,
    inbox,
    results,
    returns,
    plans,
    small_sem,
    weight_sem,
    own_sem,
    head_send,
    head_recv,
    ring_send,
    ring_recv,
    done_send,
    done_recv,
    plan_send,
    plan_recv,
    out_send,
    out_recv,
    back_send,
    back_recv,
):
    me = lax.axis_index("ctx")
    my_x = me // NY
    my_y = lax.rem(me, NY)
    rows, width = tokens.shape
    experts = router.shape[0]
    group_width = GROUP * HEAD_DIM

    def to_peer(k):
        return shifted(me, k // NY, lax.rem(k, NY))

    def from_peer(k):
        return shifted(me, -(k // NY), -lax.rem(k, NY))

    barrier = pltpu.get_barrier_semaphore()

    @pl.loop(1, PEERS)
    def _(k):
        pl.semaphore_signal(barrier, inc=1, device_id={"ctx": to_peer(k)}, device_id_type=MESH)

    smalls = [
        pltpu.make_async_copy(src, dst, small_sem.at[i])
        for i, (src, dst) in enumerate(
            ((picks_in, picks), (tokens_in, tokens), (gain_in, gain), (router_in, router))
        )
    ]
    for small in smalls:
        small.start()

    def head_columns(head):
        return pl.ds(pl.multiple_of(head * HEAD_DIM, HEAD_DIM), HEAD_DIM)

    def group_columns(head):
        return pl.ds(pl.multiple_of(head * group_width, group_width), group_width)

    own = [
        (keys.at[:, head_columns(my_x)], pairs.at[0, my_x, 0]),
        (values.at[:, head_columns(my_x)], pairs.at[0, my_x, 1]),
        (queries.at[:, group_columns(my_x)], query_rows.at[my_x]),
    ]
    own = [pltpu.make_async_copy(src, dst, own_sem.at[i]) for i, (src, dst) in enumerate(own)]
    for copy in own:
        copy.start()
    loads = [
        pltpu.make_async_copy(src, dst, weight_sem.at[i])
        for i, (src, dst) in enumerate(((w_gate, gate_w), (w_up, up_w), (w_down, down_w)))
    ]
    for load in loads:
        load.start()

    def to_head(dx, part):
        head = lax.rem(my_x + dx, NX)
        if part == 2:
            src, dst = queries.at[:, group_columns(head)], query_rows.at[my_x]
        else:
            src = (keys, values)[part].at[:, head_columns(head)]
            dst = pairs.at[0, my_x, part]
        return pltpu.make_async_remote_copy(
            src_ref=src,
            dst_ref=dst,
            send_sem=head_send.at[dx, part],
            recv_sem=head_recv.at[dx, part],
            device_id={"ctx": shifted(me, dx, 0)},
            device_id_type=MESH,
        )

    def from_head(dx, part):
        source = lax.rem(my_x - dx + NX, NX)
        dst = query_rows.at[source] if part == 2 else pairs.at[0, source, part]
        return pltpu.make_async_remote_copy(
            src_ref=dst,
            dst_ref=dst,
            send_sem=head_send.at[dx, part],
            recv_sem=head_recv.at[dx, part],
            device_id={"ctx": shifted(me, dx, 0)},
            device_id_type=MESH,
        )

    pl.semaphore_wait(barrier, PEERS - 1)
    for part in range(3):
        for dx in range(1, NX):
            to_head(dx, part).start()

    smalls[0].wait()
    picked = picks[...]
    offset = lax.rem(picked // NY - my_x + NX, NX) * NY + lax.rem(
        lax.rem(picked, NY) - my_y + NY, NY
    )
    number = lax.broadcasted_iota(jnp.int32, (PEERS, rows), 0)
    chosen = [number == offset[j : j + 1] for j in range(2)]
    either = jnp.where(chosen[0] | chosen[1], 1.0, 0.0)
    earlier = jnp.where(
        lax.broadcasted_iota(jnp.int32, (rows, rows), 0)
        < lax.broadcasted_iota(jnp.int32, (rows, rows), 1),
        1.0,
        0.0,
    ).astype(jnp.bfloat16)
    ranks = jnp.dot(either.astype(jnp.bfloat16), earlier, preferred_element_type=jnp.float32)
    place = jnp.where(either > 0.0, ranks, -1.0)
    slot = lax.broadcasted_iota(jnp.int32, (PEERS, SLOTS, rows), 1).astype(jnp.float32)
    rows_held = jnp.where(place[:, None, :] == slot, 1.0, 0.0).reshape(PEERS * SLOTS, rows)
    held[...] = rows_held.astype(jnp.bfloat16)

    def behind(step):
        return lax.select(step == 0, 0, 2 * step - 1)

    def ahead(step):
        return lax.select(step == 4, 7, 2 * step)

    def ring(up, step, i):
        block = lax.rem(my_x - i + NX, NX)
        place_of = behind if up else ahead
        way = 0 if up else 1
        return pltpu.make_async_remote_copy(
            src_ref=pairs.at[place_of(step - 1), block],
            dst_ref=pairs.at[place_of(step), block],
            send_sem=ring_send.at[way, step, i],
            recv_sem=ring_recv.at[way, step, i],
            device_id={"ctx": shifted(me, 0, 1 if up else -1)},
            device_id_type=MESH,
        )

    def forward(step, i):
        step = jnp.int32(step)

        @pl.when((step < 3) | (i < 2))
        def _():
            ring(True, step + 1, i).start()

        @pl.when((step < 3) | (i >= 2))
        def _():
            ring(False, step + 1, i).start()

    def attend(q_block, first, count, step):
        blocks = q_block + 1
        units = pairs[pl.ds(first, count), :blocks]
        key_block = units[:, :, 0].reshape(count * blocks * rows, HEAD_DIM)
        value_block = units[:, :, 1].reshape(count * blocks * rows, HEAD_DIM)
        for first_head in range(0, GROUP, HEADS_AT_ONCE):
            heads = range(first_head, first_head + HEADS_AT_ONCE)
            query = [query_rows[q_block, :, h * HEAD_DIM : (h + 1) * HEAD_DIM] for h in heads]
            query = jnp.concatenate(query, 0)
            scores = contract_last(query, key_block)
            weights = jnp.exp2(
                jnp.tanh(scores * (1.0 / (score_cap * math.sqrt(HEAD_DIM))))
                * (score_cap * math.log2(math.e))
            )
            parts = [weights[:, c : c + rows] for c in range(0, weights.shape[1], rows)]
            if step is None:
                shape = (HEADS_AT_ONCE, rows, rows)
                row = lax.broadcasted_iota(jnp.int32, shape, 1)
                column = lax.broadcasted_iota(jnp.int32, shape, 2)
                visible = [(column <= row).reshape(HEADS_AT_ONCE * rows, rows)]
            elif count == 2:
                visible = [my_y >= step, my_y >= NY - step]
            else:
                visible = [my_y >= step]
            for c, seen in enumerate(visible):
                c = c * blocks + q_block
                parts[c] = jnp.where(seen, parts[c], 0.0)
            here = pl.ds(first_head * rows, HEADS_AT_ONCE * rows)
            total = parts[0]
            for part in parts[1:]:
                total = total + part
            rounded = jnp.concatenate([part.astype(jnp.bfloat16) for part in parts], 1)
            given = jnp.dot(rounded, value_block, preferred_element_type=jnp.float32)
            if step is None:
                denoms[q_block, here] = total
                summed[q_block, here] = given
            else:
                denoms[q_block, here] += total
                summed[q_block, here] += given

    for copy in own[:2]:
        copy.wait()
    forward(0, 0)
    for dx in range(1, NX):
        from_head(dx, 0).wait_recv()
        from_head(dx, 1).wait_recv()
        forward(0, dx)
    own[2].wait()
    for dx in range(1, NX):
        from_head(dx, 2).wait_recv()

    def arrive(step, i):
        ring(True, step, i).wait_recv()
        ring(False, step, i).wait_recv()
        forward(step, i)

    for i in range(NX):
        arrive(jnp.int32(1), i)
        attend(i, 0, 1, None)

    @pl.loop(2, 4)
    def _(step):
        for i in range(NX):
            arrive(step, i)
            attend(i, 2 * step - 3, 2, step - 1)

    for i in range(NX):
        attend(i, 5, 2, 3)
        ring(i < 2, jnp.int32(4), i).wait_recv()

    def give(block):
        dx = lax.rem(block - my_x + NX, NX)
        return pltpu.make_async_remote_copy(
            src_ref=finished.at[block],
            dst_ref=attended.at[my_x],
            send_sem=done_send.at[dx],
            recv_sem=done_recv.at[dx],
            device_id={"ctx": shifted(me, dx, 0)},
            device_id_type=MESH,
        )

    def take(dx):
        source = lax.rem(my_x - dx + NX, NX)
        return pltpu.make_async_remote_copy(
            src_ref=attended.at[source],
            dst_ref=attended.at[source],
            send_sem=done_send.at[dx],
            recv_sem=done_recv.at[dx],
            device_id={"ctx": shifted(me, dx, 0)},
            device_id_type=MESH,
        )

    for block in range(NX):
        attend(block, 7, 1, 4)
        denom = jnp.sum(denoms[block], -1, keepdims=True)
        finished[block] = (
            (summed[block] / denom).astype(jnp.bfloat16).reshape(GROUP, rows, HEAD_DIM)
        )

        @pl.when(my_x != block)
        def _():
            give(block).start()

    attended[my_x] = finished[my_x]

    @pl.loop(1, NX)
    def _(dx):
        take(dx).wait_recv()

    for small in smalls[1:]:
        small.wait()
    square = jnp.zeros((rows, HEAD_DIM), jnp.float32)
    for h in range(HEADS):
        columns = slice(h * HEAD_DIM, (h + 1) * HEAD_DIM)
        stream = (
            tokens[:, columns].astype(jnp.float32)
            + attended[h // GROUP, h % GROUP].astype(jnp.float32)
        ).astype(jnp.bfloat16)
        resid[:, columns] = stream
        stream = stream.astype(jnp.float32)
        square = square + stream * stream
    mean_square = jnp.sum(square, -1, keepdims=True) / width
    normed = (
        resid[...].astype(jnp.float32)
        * lax.rsqrt(mean_square + epsilon)
        * gain[...].astype(jnp.float32).reshape(1, width)
    ).astype(jnp.bfloat16)

    def outward(k):
        return pltpu.make_async_remote_copy(
            src_ref=outbox.at[k],
            dst_ref=inbox.at[k],
            send_sem=out_send.at[k],
            recv_sem=out_recv.at[k],
            device_id={"ctx": to_peer(k)},
            device_id_type=MESH,
        )

    def backward(k):
        return pltpu.make_async_remote_copy(
            src_ref=results.at[k],
            dst_ref=returns.at[k],
            send_sem=back_send.at[k],
            recv_sem=back_recv.at[k],
            device_id={"ctx": from_peer(k)},
            device_id_type=MESH,
        )

    for chunk in range(NX):
        first = chunk * NY
        packed = jnp.dot(
            held[first * SLOTS : (first + NY) * SLOTS], normed, preferred_element_type=jnp.float32
        )
        packed = packed.astype(jnp.bfloat16).reshape(NY, SLOTS, width)
        outbox[first : first + NY] = packed
        if chunk == 0:
            inbox[0] = packed[0]

        @pl.loop(max(first, 1), first + NY)
        def _(k):
            outward(k).start()

    logits = logit_cap * jnp.tanh(contract_last(router[...], normed) / logit_cap)
    plan = jnp.exp(logits)
    plan = plan / jnp.sum(plan, 0, keepdims=True)
    plans[0] = plan.astype(jnp.bfloat16)

    def plan_column(dy):
        return pltpu.make_async_remote_copy(
            src_ref=plans.at[0],
            dst_ref=plans.at[dy],
            send_sem=plan_send.at[dy],
            recv_sem=plan_recv.at[dy],
            device_id={"ctx": shifted(me, 0, dy)},
            device_id_type=MESH,
        )

    def plan_row(dx):
        return pltpu.make_async_remote_copy(
            src_ref=plans.at[pl.ds(0, NY)],
            dst_ref=plans.at[pl.ds(dx * NY, NY)],
            send_sem=plan_send.at[NY + dx],
            recv_sem=plan_recv.at[NY + dx],
            device_id={"ctx": shifted(me, dx, 0)},
            device_id_type=MESH,
        )

    for dy in range(1, NY):
        plan_column(dy).start()

    for load in loads:
        load.wait()

    @pl.loop(0, NX)
    def _(chunk):
        first = chunk * NY

        @pl.loop(jnp.maximum(first, 1), first + NY)
        def _(k):
            outward(k).wait_recv()

        block = inbox[pl.ds(first, NY)].reshape(NY * SLOTS, width)
        gate = jnp.dot(block, gate_w[...], preferred_element_type=jnp.float32)
        upward = jnp.dot(block, up_w[...], preferred_element_type=jnp.float32)
        hidden = (gate / (1.0 + jnp.exp(-gate)) * upward).astype(jnp.bfloat16)
        given = jnp.dot(hidden, down_w[...], preferred_element_type=jnp.float32)
        results[pl.ds(first, NY)] = given.astype(jnp.bfloat16).reshape(NY, SLOTS, width)

        @pl.loop(jnp.maximum(first, 1), first + NY)
        def _(k):
            backward(k).start()

        @pl.when(chunk == 1)
        def _():
            for dy in range(1, NY):
                plan_column(dy).wait_recv()
            for dx in range(1, NX):
                plan_row(dx).start()

    returns[0] = results[0]

    for dx in range(1, NX):
        plan_row(dx).wait_recv()

    target = float(rows * PEERS * 2 / experts)

    def column_sums(scale):
        def add(s, total):
            block = plans[s].astype(jnp.float32)
            if scale is None:
                return total + block
            return total + block * (2.0 / jnp.sum(block * scale, 0, keepdims=True))

        total = lax.fori_loop(0, PEERS, add, jnp.zeros((experts, rows), jnp.float32), unroll=4)
        return jnp.sum(total, 1, keepdims=True)

    scale = target / column_sums(None)
    scale = lax.fori_loop(0, ITERS - 1, lambda _, s: target / column_sums(s), scale)
    plan = plan * scale
    plan = plan * (2.0 / jnp.sum(plan, 0, keepdims=True))
    named = lax.broadcasted_iota(jnp.int32, (experts, rows), 0)
    mass = [
        jnp.sum(jnp.where(named == picked[j : j + 1], plan, 0.0), 0, keepdims=True)
        for j in range(2)
    ]
    total = mass[0] + mass[1]
    gates = jnp.where(chosen[0], mass[0] / total, 0.0) + jnp.where(chosen[1], mass[1] / total, 0.0)
    mixing = jnp.where(place[:, None, :] == slot, gates[:, None, :], 0.0)
    mixing = mixing.reshape(PEERS * SLOTS, rows).T
    high = mixing.astype(jnp.bfloat16)
    low = (mixing - high.astype(jnp.float32)).astype(jnp.bfloat16)

    @pl.loop(1, PEERS)
    def _(k):
        backward(k).wait_recv()

    step = 512
    for first in range(0, width, step):
        columns = pl.ds(first, step)
        block = returns[:, :, columns].reshape(PEERS * SLOTS, step)
        mixture = jnp.dot(high, block, preferred_element_type=jnp.float32) + jnp.dot(
            low, block, preferred_element_type=jnp.float32
        )
        layer[:, columns] = (resid[:, columns].astype(jnp.float32) + mixture).astype(jnp.bfloat16)

    for part in range(3):
        for dx in range(1, NX):
            to_head(dx, part).wait_send()

    @pl.loop(1, 4)
    def _(step):
        @pl.loop(0, NX)
        def _(i):
            ring(True, step, i).wait_send()
            ring(False, step, i).wait_send()

    @pl.loop(0, 2)
    def _(i):
        ring(True, jnp.int32(4), i).wait_send()
        ring(False, jnp.int32(4), i + 2).wait_send()

    @pl.loop(1, NX)
    def _(dx):
        give(lax.rem(my_x + dx, NX)).wait_send()

    @pl.loop(1, PEERS)
    def _(k):
        outward(k).wait_send()
        backward(k).wait_send()

    for dy in range(1, NY):
        plan_column(dy).wait_send()
    for dx in range(1, NX):
        plan_row(dx).wait_send()


def per_device(tokens, queries, keys, values, norm_gain, router, w_gate, w_up, w_down, picks):
    rows, width = tokens.shape
    hidden = w_gate.shape[-1]
    experts = router.shape[1]
    whole = pl.BlockSpec(memory_space=pltpu.VMEM)
    apart = pl.BlockSpec(memory_space=pltpu.HBM)
    box = pltpu.VMEM((PEERS, SLOTS, width), jnp.bfloat16)
    sems = pltpu.SemaphoreType.DMA
    heads_of_block = pltpu.VMEM((NX, GROUP, rows, HEAD_DIM), jnp.bfloat16)
    running = pltpu.VMEM((NX, GROUP * rows, HEAD_DIM), jnp.float32)
    return pl.pallas_call(
        layer_kernel,
        out_shape=jax.ShapeDtypeStruct((rows, width), jnp.bfloat16),
        in_specs=[apart] * 10,
        out_specs=whole,
        scratch_shapes=[
            pltpu.VMEM((rows, width), jnp.bfloat16),
            pltpu.VMEM((width,), jnp.bfloat16),
            pltpu.VMEM((experts, width), jnp.bfloat16),
            pltpu.VMEM((2, rows), jnp.int32),
            pltpu.VMEM((width, hidden), jnp.bfloat16),
            pltpu.VMEM((width, hidden), jnp.bfloat16),
            pltpu.VMEM((hidden, width), jnp.bfloat16),
            pltpu.VMEM((NX, rows, GROUP * HEAD_DIM), jnp.bfloat16),
            pltpu.VMEM((NY, NX, 2, rows, HEAD_DIM), jnp.bfloat16),
            running,
            running,
            heads_of_block,
            heads_of_block,
            pltpu.VMEM((rows, width), jnp.bfloat16),
            pltpu.VMEM((PEERS * SLOTS, rows), jnp.bfloat16),
            box,
            box,
            box,
            box,
            pltpu.VMEM((PEERS, experts, rows), jnp.bfloat16),
            sems((4,)),
            sems((3,)),
            sems((3,)),
            sems((NX, 3)),
            sems((NX, 3)),
            sems((2, 5, NX)),
            sems((2, 5, NX)),
            sems((NX,)),
            sems((NX,)),
            sems((NY + NX,)),
            sems((NY + NX,)),
            sems((PEERS,)),
            sems((PEERS,)),
            sems((PEERS,)),
            sems((PEERS,)),
        ],
        compiler_params=pltpu.CompilerParams(
            collective_id=1, has_side_effects=True, vmem_limit_bytes=VMEM_LIMIT
        ),
        name="layer",
    )(
        tokens,
        norm_gain,
        router.T,
        picks.T,
        queries,
        keys,
        values,
        w_gate[0],
        w_up[0],
        w_down[0],
    )


def solution(mesh):
    placed = (
        P(("seq", "ctx"), None),
        P(("seq", "ctx"), None),
        P(("seq", "ctx"), None),
        P(("seq", "ctx"), None),
        P(),
        P(),
        P("ctx", None, None),
        P("ctx", None, None),
        P("ctx", None, None),
        P(("seq", "ctx"), None),
    )
    return jax.shard_map(
        per_device, mesh=mesh, in_specs=placed, out_specs=P(("seq", "ctx"), None), check_vma=False
    )
```

```python
import math

import jax
import jax.numpy as jnp
from jax import lax
from jax.experimental import pallas as pl
from jax.experimental.pallas import tpu as pltpu
from jax.sharding import PartitionSpec as P

HEADS = 16
KV_HEADS = 4
GROUP = HEADS // KV_HEADS
HEAD_DIM = 128
ITERS = 8
MESH = pl.DeviceIdType.MESH
NX = 4
NY = 8
PEERS = NX * NY
SLOTS = 8
MIX_WIDTH = 512
HEADS_AT_ONCE = 4
VMEM_LIMIT = 60 * 1024 * 1024


score_cap = 50.0
logit_cap = 10.0
epsilon = 1e-06


def shifted(me, dx, dy):
    return lax.rem(me // NY + dx + NX, NX) * NY + lax.rem(lax.rem(me, NY) + dy + NY, NY)


def contract_last(left, right):
    return lax.dot_general(
        left, right, (((1,), (1,)), ((), ())), preferred_element_type=jnp.float32
    )


def layer_kernel(
    tokens_in,
    gain_in,
    router_in,
    picks_in,
    queries,
    keys,
    values,
    w_gate,
    w_up,
    w_down,
    layer,
    tokens,
    gain,
    router,
    picks,
    gate_w,
    up_w,
    down_w,
    query_rows,
    pairs,
    summed,
    denoms,
    finished,
    attended,
    resid,
    held,
    mixed,
    outbox,
    inbox,
    results,
    returns,
    plans,
    small_sem,
    weight_sem,
    own_sem,
    head_send,
    head_recv,
    ring_send,
    ring_recv,
    done_send,
    done_recv,
    plan_send,
    plan_recv,
    out_send,
    out_recv,
    back_send,
    back_recv,
):
    me = lax.axis_index("ctx")
    my_x = me // NY
    my_y = lax.rem(me, NY)
    rows, width = tokens.shape
    experts = router.shape[0]
    group_width = GROUP * HEAD_DIM

    def to_peer(k):
        return shifted(me, k // NY, lax.rem(k, NY))

    def from_peer(k):
        return shifted(me, -(k // NY), -lax.rem(k, NY))

    barrier = pltpu.get_barrier_semaphore()

    near = [shifted(me, dx, 0) for dx in range(1, NX)] + [shifted(me, 0, dy) for dy in (1, -1)]
    for peer in near:
        pl.semaphore_signal(barrier, inc=1, device_id={"ctx": peer}, device_id_type=MESH)

    smalls = [
        pltpu.make_async_copy(src, dst, small_sem.at[i])
        for i, (src, dst) in enumerate(
            ((picks_in, picks), (tokens_in, tokens), (gain_in, gain), (router_in, router))
        )
    ]
    for small in smalls:
        small.start()

    def head_columns(head):
        return pl.ds(pl.multiple_of(head * HEAD_DIM, HEAD_DIM), HEAD_DIM)

    def group_columns(head):
        return pl.ds(pl.multiple_of(head * group_width, group_width), group_width)

    own = [
        (keys.at[:, head_columns(my_x)], pairs.at[0, my_x, 0]),
        (values.at[:, head_columns(my_x)], pairs.at[0, my_x, 1]),
        (queries.at[:, group_columns(my_x)], query_rows.at[my_x]),
    ]
    own = [pltpu.make_async_copy(src, dst, own_sem.at[i]) for i, (src, dst) in enumerate(own)]
    for copy in own:
        copy.start()
    loads = [
        pltpu.make_async_copy(src, dst, weight_sem.at[i])
        for i, (src, dst) in enumerate(((w_gate, gate_w), (w_up, up_w), (w_down, down_w)))
    ]
    for load in loads:
        load.start()

    def to_head(dx, part):
        head = lax.rem(my_x + dx, NX)
        if part == 2:
            src, dst = queries.at[:, group_columns(head)], query_rows.at[my_x]
        else:
            src = (keys, values)[part].at[:, head_columns(head)]
            dst = pairs.at[0, my_x, part]
        return pltpu.make_async_remote_copy(
            src_ref=src,
            dst_ref=dst,
            send_sem=head_send.at[dx, part],
            recv_sem=head_recv.at[dx, part],
            device_id={"ctx": shifted(me, dx, 0)},
            device_id_type=MESH,
        )

    def from_head(dx, part):
        source = lax.rem(my_x - dx + NX, NX)
        dst = query_rows.at[source] if part == 2 else pairs.at[0, source, part]
        return pltpu.make_async_remote_copy(
            src_ref=dst,
            dst_ref=dst,
            send_sem=head_send.at[dx, part],
            recv_sem=head_recv.at[dx, part],
            device_id={"ctx": shifted(me, dx, 0)},
            device_id_type=MESH,
        )

    pl.semaphore_wait(barrier, len(near))
    for dx in range(1, NX):
        for part in range(2):
            to_head(dx, part).start()

    smalls[0].wait()
    picked = picks[...]
    offset = lax.rem(picked // NY - my_x + NX, NX) * NY + lax.rem(
        lax.rem(picked, NY) - my_y + NY, NY
    )
    number = lax.broadcasted_iota(jnp.int32, (PEERS, rows), 0)
    chosen = [number == offset[j : j + 1] for j in range(2)]
    either = jnp.where(chosen[0] | chosen[1], 1.0, 0.0)
    earlier = jnp.where(
        lax.broadcasted_iota(jnp.int32, (rows, rows), 0)
        < lax.broadcasted_iota(jnp.int32, (rows, rows), 1),
        1.0,
        0.0,
    ).astype(jnp.bfloat16)
    ranks = jnp.dot(either.astype(jnp.bfloat16), earlier, preferred_element_type=jnp.float32)
    place = jnp.where(either > 0.0, ranks, -1.0)
    slot = lax.broadcasted_iota(jnp.int32, (PEERS, SLOTS, rows), 1).astype(jnp.float32)
    rows_held = jnp.where(place[:, None, :] == slot, 1.0, 0.0).reshape(PEERS * SLOTS, rows)
    held[...] = rows_held.astype(jnp.bfloat16)

    def behind(step):
        return lax.select(step == 0, 0, 2 * step - 1)

    def ahead(step):
        return lax.select(step == 4, 7, 2 * step)

    def ring(up, step, i):
        block = lax.rem(my_x - i + NX, NX)
        place_of = behind if up else ahead
        way = 0 if up else 1
        return pltpu.make_async_remote_copy(
            src_ref=pairs.at[place_of(step - 1), block],
            dst_ref=pairs.at[place_of(step), block],
            send_sem=ring_send.at[way, step, i],
            recv_sem=ring_recv.at[way, step, i],
            device_id={"ctx": shifted(me, 0, 1 if up else -1)},
            device_id_type=MESH,
        )

    def forward(step, i):
        step = jnp.int32(step)

        @pl.when((step < 3) | (i < 2))
        def _():
            ring(True, step + 1, i).start()

        @pl.when((step < 3) | (i >= 2))
        def _():
            ring(False, step + 1, i).start()

    def attend(q_block, first, count, step):
        blocks = q_block + 1
        units = pairs[pl.ds(first, count), :blocks]
        key_block = units[:, :, 0].reshape(count * blocks * rows, HEAD_DIM)
        value_block = units[:, :, 1].reshape(count * blocks * rows, HEAD_DIM)
        for first_head in range(0, GROUP, HEADS_AT_ONCE):
            heads = range(first_head, first_head + HEADS_AT_ONCE)
            query = [query_rows[q_block, :, h * HEAD_DIM : (h + 1) * HEAD_DIM] for h in heads]
            query = jnp.concatenate(query, 0)
            scores = contract_last(query, key_block)
            weights = jnp.exp2(
                jnp.tanh(scores * (1.0 / (score_cap * math.sqrt(HEAD_DIM))))
                * (score_cap * math.log2(math.e))
            )
            parts = [weights[:, c : c + rows] for c in range(0, weights.shape[1], rows)]
            if step is None:
                shape = (HEADS_AT_ONCE, rows, rows)
                row = lax.broadcasted_iota(jnp.int32, shape, 1)
                column = lax.broadcasted_iota(jnp.int32, shape, 2)
                visible = [(column <= row).reshape(HEADS_AT_ONCE * rows, rows)]
            elif count == 2:
                visible = [my_y >= step, my_y >= NY - step]
            else:
                visible = [my_y >= step]
            for c, seen in enumerate(visible):
                c = c * blocks + q_block
                parts[c] = jnp.where(seen, parts[c], 0.0)
            here = pl.ds(first_head * rows, HEADS_AT_ONCE * rows)
            total = parts[0]
            for part in parts[1:]:
                total = total + part
            rounded = jnp.concatenate([part.astype(jnp.bfloat16) for part in parts], 1)
            given = jnp.dot(rounded, value_block, preferred_element_type=jnp.float32)
            if step is None:
                denoms[q_block, here] = total
                summed[q_block, here] = given
            else:
                denoms[q_block, here] += total
                summed[q_block, here] += given

    for copy in own[:2]:
        copy.wait()
    forward(0, 0)
    for dx in range(1, NX):
        from_head(dx, 0).wait_recv()
        from_head(dx, 1).wait_recv()
        forward(0, dx)
    for dx in range(1, NX):
        to_head(dx, 2).start()
    own[2].wait()
    for dx in range(1, NX):
        from_head(dx, 2).wait_recv()

    def arrive(step, i):
        ring(True, step, i).wait_recv()
        ring(False, step, i).wait_recv()
        forward(step, i)

    for i in range(NX):
        arrive(jnp.int32(1), i)
        attend(i, 0, 1, None)

    @pl.loop(2, 4)
    def _(step):
        for i in range(NX):
            arrive(step, i)
            attend(i, 2 * step - 3, 2, step - 1)

    for i in range(NX):
        attend(i, 5, 2, 3)
        ring(i < 2, jnp.int32(4), i).wait_recv()

    def give(block):
        dx = lax.rem(block - my_x + NX, NX)
        return pltpu.make_async_remote_copy(
            src_ref=finished.at[block],
            dst_ref=attended.at[my_x],
            send_sem=done_send.at[dx],
            recv_sem=done_recv.at[dx],
            device_id={"ctx": shifted(me, dx, 0)},
            device_id_type=MESH,
        )

    def take(dx):
        source = lax.rem(my_x - dx + NX, NX)
        return pltpu.make_async_remote_copy(
            src_ref=attended.at[source],
            dst_ref=attended.at[source],
            send_sem=done_send.at[dx],
            recv_sem=done_recv.at[dx],
            device_id={"ctx": shifted(me, dx, 0)},
            device_id_type=MESH,
        )

    for block in range(NX):
        attend(block, 7, 1, 4)
        denom = jnp.sum(denoms[block], -1, keepdims=True)
        finished[block] = (
            (summed[block] / denom).astype(jnp.bfloat16).reshape(GROUP, rows, HEAD_DIM)
        )

        @pl.when(my_x != block)
        def _():
            give(block).start()

    attended[my_x] = finished[my_x]

    @pl.loop(1, NX)
    def _(dx):
        take(dx).wait_recv()

    for small in smalls[1:]:
        small.wait()
    square = jnp.zeros((rows, HEAD_DIM), jnp.float32)
    for h in range(HEADS):
        columns = slice(h * HEAD_DIM, (h + 1) * HEAD_DIM)
        stream = (
            tokens[:, columns].astype(jnp.float32)
            + attended[h // GROUP, h % GROUP].astype(jnp.float32)
        ).astype(jnp.bfloat16)
        resid[:, columns] = stream
        stream = stream.astype(jnp.float32)
        square = square + stream * stream
    mean_square = jnp.sum(square, -1, keepdims=True) / width
    normed = (
        resid[...].astype(jnp.float32)
        * lax.rsqrt(mean_square + epsilon)
        * gain[...].astype(jnp.float32).reshape(1, width)
    ).astype(jnp.bfloat16)

    def outward(k):
        return pltpu.make_async_remote_copy(
            src_ref=outbox.at[k],
            dst_ref=inbox.at[k],
            send_sem=out_send.at[k],
            recv_sem=out_recv.at[k],
            device_id={"ctx": to_peer(k)},
            device_id_type=MESH,
        )

    def backward(k):
        return pltpu.make_async_remote_copy(
            src_ref=results.at[k],
            dst_ref=returns.at[k],
            send_sem=back_send.at[k],
            recv_sem=back_recv.at[k],
            device_id={"ctx": from_peer(k)},
            device_id_type=MESH,
        )

    for chunk in range(NX):
        first = chunk * NY
        packed = jnp.dot(
            held[first * SLOTS : (first + NY) * SLOTS], normed, preferred_element_type=jnp.float32
        )
        packed = packed.astype(jnp.bfloat16).reshape(NY, SLOTS, width)
        outbox[first : first + NY] = packed
        if chunk == 0:
            inbox[0] = packed[0]

        @pl.loop(max(first, 1), first + NY)
        def _(k):
            outward(k).start()

    logits = logit_cap * jnp.tanh(contract_last(router[...], normed) / logit_cap)
    plan = jnp.exp(logits)
    plan = plan / jnp.sum(plan, 0, keepdims=True)
    plans[0] = plan.astype(jnp.bfloat16)

    def plan_column(dy):
        return pltpu.make_async_remote_copy(
            src_ref=plans.at[0],
            dst_ref=plans.at[dy],
            send_sem=plan_send.at[dy],
            recv_sem=plan_recv.at[dy],
            device_id={"ctx": shifted(me, 0, dy)},
            device_id_type=MESH,
        )

    def plan_row(dx):
        return pltpu.make_async_remote_copy(
            src_ref=plans.at[pl.ds(0, NY)],
            dst_ref=plans.at[pl.ds(dx * NY, NY)],
            send_sem=plan_send.at[NY + dx],
            recv_sem=plan_recv.at[NY + dx],
            device_id={"ctx": shifted(me, dx, 0)},
            device_id_type=MESH,
        )

    for dy in range(1, NY):
        plan_column(dy).start()

    for load in loads:
        load.wait()

    @pl.loop(0, NX)
    def _(chunk):
        first = chunk * NY

        @pl.loop(jnp.maximum(first, 1), first + NY)
        def _(k):
            outward(k).wait_recv()

        block = inbox[pl.ds(first, NY)].reshape(NY * SLOTS, width)
        gate = jnp.dot(block, gate_w[...], preferred_element_type=jnp.float32)
        upward = jnp.dot(block, up_w[...], preferred_element_type=jnp.float32)
        hidden = (gate / (1.0 + jnp.exp(-gate)) * upward).astype(jnp.bfloat16)
        given = jnp.dot(hidden, down_w[...], preferred_element_type=jnp.float32)
        results[pl.ds(first, NY)] = given.astype(jnp.bfloat16).reshape(NY, SLOTS, width)

        @pl.loop(jnp.maximum(first, 1), first + NY)
        def _(k):
            backward(k).start()

        @pl.when(chunk == 1)
        def _():
            for dy in range(1, NY):
                plan_column(dy).wait_recv()
            for dx in range(1, NX):
                plan_row(dx).start()

    returns[0] = results[0]

    for dx in range(1, NX):
        plan_row(dx).wait_recv()

    target = float(rows * PEERS * 2 / experts)

    def column_sums(scale):
        def add(s, total):
            block = plans[s].astype(jnp.float32)
            if scale is None:
                return total + block
            return total + block * (2.0 / jnp.sum(block * scale, 0, keepdims=True))

        total = lax.fori_loop(0, PEERS, add, jnp.zeros((experts, rows), jnp.float32), unroll=4)
        return jnp.sum(total, 1, keepdims=True)

    scale = target / column_sums(None)
    scale = lax.fori_loop(0, ITERS - 1, lambda _, s: target / column_sums(s), scale)
    plan = plan * scale
    plan = plan * (2.0 / jnp.sum(plan, 0, keepdims=True))
    named = lax.broadcasted_iota(jnp.int32, (experts, rows), 0)
    mass = [
        jnp.sum(jnp.where(named == picked[j : j + 1], plan, 0.0), 0, keepdims=True)
        for j in range(2)
    ]
    total = mass[0] + mass[1]
    gates = jnp.where(chosen[0], mass[0] / total, 0.0) + jnp.where(chosen[1], mass[1] / total, 0.0)
    mixing = jnp.where(place[:, None, :] == slot, gates[:, None, :], 0.0)
    mixing = mixing.reshape(PEERS * SLOTS, rows).T
    high = mixing.astype(jnp.bfloat16)
    low = (mixing - high.astype(jnp.float32)).astype(jnp.bfloat16)

    for part in range(3):
        for dx in range(1, NX):
            to_head(dx, part).wait_send()

    @pl.loop(1, 4)
    def _(step):
        @pl.loop(0, NX)
        def _(i):
            ring(True, step, i).wait_send()
            ring(False, step, i).wait_send()

    @pl.loop(0, 2)
    def _(i):
        ring(True, jnp.int32(4), i).wait_send()
        ring(False, jnp.int32(4), i + 2).wait_send()

    @pl.loop(1, NX)
    def _(dx):
        give(lax.rem(my_x + dx, NX)).wait_send()

    @pl.loop(1, PEERS)
    def _(k):
        outward(k).wait_send()

    for dy in range(1, NY):
        plan_column(dy).wait_send()
    for dx in range(1, NX):
        plan_row(dx).wait_send()

    def mix(k, first, last):
        columns = pl.ds(first, MIX_WIDTH)
        block = returns[k:last, :, columns].reshape((last - k) * SLOTS, MIX_WIDTH)
        here = slice(k * SLOTS, last * SLOTS)
        return jnp.dot(high[:, here], block, preferred_element_type=jnp.float32) + jnp.dot(
            low[:, here], block, preferred_element_type=jnp.float32
        )

    most = PEERS // 2

    @pl.loop(1, most)
    def _(k):
        backward(k).wait_recv()

    for first in range(0, width, MIX_WIDTH):
        columns = pl.ds(first, MIX_WIDTH)
        mixed[:, columns] = resid[:, columns].astype(jnp.float32) + mix(0, first, most)

    @pl.loop(most, PEERS)
    def _(k):
        backward(k).wait_recv()

    for first in range(0, width, MIX_WIDTH):
        columns = pl.ds(first, MIX_WIDTH)
        layer[:, columns] = (mixed[:, columns] + mix(most, first, PEERS)).astype(jnp.bfloat16)

    @pl.loop(1, PEERS)
    def _(k):
        backward(k).wait_send()


def per_device(tokens, queries, keys, values, norm_gain, router, w_gate, w_up, w_down, picks):
    rows, width = tokens.shape
    hidden = w_gate.shape[-1]
    experts = router.shape[1]
    whole = pl.BlockSpec(memory_space=pltpu.VMEM)
    apart = pl.BlockSpec(memory_space=pltpu.HBM)
    box = pltpu.VMEM((PEERS, SLOTS, width), jnp.bfloat16)
    sems = pltpu.SemaphoreType.DMA
    heads_of_block = pltpu.VMEM((NX, GROUP, rows, HEAD_DIM), jnp.bfloat16)
    running = pltpu.VMEM((NX, GROUP * rows, HEAD_DIM), jnp.float32)
    return pl.pallas_call(
        layer_kernel,
        out_shape=jax.ShapeDtypeStruct((rows, width), jnp.bfloat16),
        in_specs=[apart] * 10,
        out_specs=whole,
        scratch_shapes=[
            pltpu.VMEM((rows, width), jnp.bfloat16),
            pltpu.VMEM((width,), jnp.bfloat16),
            pltpu.VMEM((experts, width), jnp.bfloat16),
            pltpu.VMEM((2, rows), jnp.int32),
            pltpu.VMEM((width, hidden), jnp.bfloat16),
            pltpu.VMEM((width, hidden), jnp.bfloat16),
            pltpu.VMEM((hidden, width), jnp.bfloat16),
            pltpu.VMEM((NX, rows, GROUP * HEAD_DIM), jnp.bfloat16),
            pltpu.VMEM((NY, NX, 2, rows, HEAD_DIM), jnp.bfloat16),
            running,
            running,
            heads_of_block,
            heads_of_block,
            pltpu.VMEM((rows, width), jnp.bfloat16),
            pltpu.VMEM((PEERS * SLOTS, rows), jnp.bfloat16),
            pltpu.VMEM((rows, width), jnp.float32),
            box,
            box,
            box,
            box,
            pltpu.VMEM((PEERS, experts, rows), jnp.bfloat16),
            sems((4,)),
            sems((3,)),
            sems((3,)),
            sems((NX, 3)),
            sems((NX, 3)),
            sems((2, 5, NX)),
            sems((2, 5, NX)),
            sems((NX,)),
            sems((NX,)),
            sems((NY + NX,)),
            sems((NY + NX,)),
            sems((PEERS,)),
            sems((PEERS,)),
            sems((PEERS,)),
            sems((PEERS,)),
        ],
        compiler_params=pltpu.CompilerParams(
            collective_id=1, has_side_effects=True, vmem_limit_bytes=VMEM_LIMIT
        ),
        name="layer",
    )(
        tokens,
        norm_gain,
        router.T,
        picks.T,
        queries,
        keys,
        values,
        w_gate[0],
        w_up[0],
        w_down[0],
    )


def solution(mesh):
    placed = (
        P(("seq", "ctx"), None),
        P(("seq", "ctx"), None),
        P(("seq", "ctx"), None),
        P(("seq", "ctx"), None),
        P(),
        P(),
        P("ctx", None, None),
        P("ctx", None, None),
        P("ctx", None, None),
        P(("seq", "ctx"), None),
    )
    return jax.shard_map(
        per_device, mesh=mesh, in_specs=placed, out_specs=P(("seq", "ctx"), None), check_vma=False
    )
```

```python
import math

import jax
import jax.numpy as jnp
from jax import lax
from jax.experimental import pallas as pl
from jax.experimental.pallas import tpu as pltpu
from jax.sharding import PartitionSpec as P

HEADS = 16
KV_HEADS = 4
GROUP = HEADS // KV_HEADS
HEAD_DIM = 128
ITERS = 8
MESH = pl.DeviceIdType.MESH
NX = 4
NY = 8
PEERS = NX * NY
SLOTS = 8
MIX_WIDTH = 512
HEADS_AT_ONCE = 4
VMEM_LIMIT = 60 * 1024 * 1024


score_cap = 50.0
logit_cap = 10.0
epsilon = 1e-06


def shifted(me, dx, dy):
    return lax.rem(me // NY + dx + NX, NX) * NY + lax.rem(lax.rem(me, NY) + dy + NY, NY)


def contract_last(left, right):
    return lax.dot_general(
        left, right, (((1,), (1,)), ((), ())), preferred_element_type=jnp.float32
    )


def layer_kernel(
    tokens_in,
    gain_in,
    router_in,
    picks_in,
    queries,
    keys,
    values,
    w_gate,
    w_up,
    w_down,
    layer,
    tokens,
    gain,
    router,
    picks,
    gate_w,
    up_w,
    down_w,
    query_rows,
    pairs,
    summed,
    denoms,
    finished,
    attended,
    resid,
    held,
    mixed,
    first_out,
    rest_out,
    first_in,
    rest_in,
    landed,
    results,
    returns,
    plans,
    small_sem,
    weight_sem,
    own_sem,
    head_send,
    head_recv,
    ring_send,
    ring_recv,
    done_send,
    done_recv,
    plan_send,
    plan_recv,
    out_send,
    out_recv,
    back_send,
    back_recv,
):
    me = lax.axis_index("ctx")
    my_x = me // NY
    my_y = lax.rem(me, NY)
    rows, width = tokens.shape
    experts = router.shape[0]
    group_width = GROUP * HEAD_DIM

    def to_peer(k):
        return shifted(me, k // NY, lax.rem(k, NY))

    def from_peer(k):
        return shifted(me, -(k // NY), -lax.rem(k, NY))

    barrier = pltpu.get_barrier_semaphore()

    near = [shifted(me, dx, 0) for dx in range(1, NX)] + [shifted(me, 0, dy) for dy in (1, -1)]
    for peer in near:
        pl.semaphore_signal(barrier, inc=1, device_id={"ctx": peer}, device_id_type=MESH)

    smalls = [
        pltpu.make_async_copy(src, dst, small_sem.at[i])
        for i, (src, dst) in enumerate(
            ((picks_in, picks), (tokens_in, tokens), (gain_in, gain), (router_in, router))
        )
    ]
    for small in smalls:
        small.start()

    def head_columns(head):
        return pl.ds(pl.multiple_of(head * HEAD_DIM, HEAD_DIM), HEAD_DIM)

    def group_columns(head):
        return pl.ds(pl.multiple_of(head * group_width, group_width), group_width)

    own = [
        (keys.at[:, head_columns(my_x)], pairs.at[0, my_x, 0]),
        (values.at[:, head_columns(my_x)], pairs.at[0, my_x, 1]),
        (queries.at[:, group_columns(my_x)], query_rows.at[my_x]),
    ]
    own = [pltpu.make_async_copy(src, dst, own_sem.at[i]) for i, (src, dst) in enumerate(own)]
    for copy in own:
        copy.start()
    loads = [
        pltpu.make_async_copy(src, dst, weight_sem.at[i])
        for i, (src, dst) in enumerate(((w_gate, gate_w), (w_up, up_w), (w_down, down_w)))
    ]
    for load in loads:
        load.start()

    def to_head(dx, part):
        head = lax.rem(my_x + dx, NX)
        if part == 2:
            src, dst = queries.at[:, group_columns(head)], query_rows.at[my_x]
        else:
            src = (keys, values)[part].at[:, head_columns(head)]
            dst = pairs.at[0, my_x, part]
        return pltpu.make_async_remote_copy(
            src_ref=src,
            dst_ref=dst,
            send_sem=head_send.at[dx, part],
            recv_sem=head_recv.at[dx, part],
            device_id={"ctx": shifted(me, dx, 0)},
            device_id_type=MESH,
        )

    def from_head(dx, part):
        source = lax.rem(my_x - dx + NX, NX)
        dst = query_rows.at[source] if part == 2 else pairs.at[0, source, part]
        return pltpu.make_async_remote_copy(
            src_ref=dst,
            dst_ref=dst,
            send_sem=head_send.at[dx, part],
            recv_sem=head_recv.at[dx, part],
            device_id={"ctx": shifted(me, dx, 0)},
            device_id_type=MESH,
        )

    pl.semaphore_wait(barrier, len(near))
    for dx in range(1, NX):
        for part in range(2):
            to_head(dx, part).start()

    smalls[0].wait()
    picked = picks[...]
    offset = lax.rem(picked // NY - my_x + NX, NX) * NY + lax.rem(
        lax.rem(picked, NY) - my_y + NY, NY
    )
    number = lax.broadcasted_iota(jnp.int32, (PEERS, rows), 0)
    chosen = [number == offset[j : j + 1] for j in range(2)]
    either = jnp.where(chosen[0] | chosen[1], 1.0, 0.0)
    earlier = jnp.where(
        lax.broadcasted_iota(jnp.int32, (rows, rows), 0)
        < lax.broadcasted_iota(jnp.int32, (rows, rows), 1),
        1.0,
        0.0,
    ).astype(jnp.bfloat16)
    ranks = jnp.dot(either.astype(jnp.bfloat16), earlier, preferred_element_type=jnp.float32)
    place = jnp.where(either > 0.0, ranks, -1.0)
    slot = lax.broadcasted_iota(jnp.int32, (PEERS, SLOTS, rows), 1).astype(jnp.float32)
    rows_held = jnp.where(place[:, None, :] == slot, 1.0, 0.0).reshape(PEERS * SLOTS, rows)
    held[...] = rows_held.astype(jnp.bfloat16)

    def behind(step):
        return lax.select(step == 0, 0, 2 * step - 1)

    def ahead(step):
        return lax.select(step == 4, 7, 2 * step)

    def ring(up, step, i):
        block = lax.rem(my_x - i + NX, NX)
        place_of = behind if up else ahead
        way = 0 if up else 1
        return pltpu.make_async_remote_copy(
            src_ref=pairs.at[place_of(step - 1), block],
            dst_ref=pairs.at[place_of(step), block],
            send_sem=ring_send.at[way, step, i],
            recv_sem=ring_recv.at[way, step, i],
            device_id={"ctx": shifted(me, 0, 1 if up else -1)},
            device_id_type=MESH,
        )

    def forward(step, i):
        step = jnp.int32(step)

        @pl.when((step < 3) | (i < 2))
        def _():
            ring(True, step + 1, i).start()

        @pl.when((step < 3) | (i >= 2))
        def _():
            ring(False, step + 1, i).start()

    def attend(q_block, first, count, step):
        blocks = q_block + 1
        units = pairs[pl.ds(first, count), :blocks]
        key_block = units[:, :, 0].reshape(count * blocks * rows, HEAD_DIM)
        value_block = units[:, :, 1].reshape(count * blocks * rows, HEAD_DIM)
        for first_head in range(0, GROUP, HEADS_AT_ONCE):
            heads = range(first_head, first_head + HEADS_AT_ONCE)
            query = [query_rows[q_block, :, h * HEAD_DIM : (h + 1) * HEAD_DIM] for h in heads]
            query = jnp.concatenate(query, 0)
            scores = contract_last(query, key_block)
            weights = jnp.exp2(
                jnp.tanh(scores * (1.0 / (score_cap * math.sqrt(HEAD_DIM))))
                * (score_cap * math.log2(math.e))
            )
            parts = [weights[:, c : c + rows] for c in range(0, weights.shape[1], rows)]
            if step is None:
                shape = (HEADS_AT_ONCE, rows, rows)
                row = lax.broadcasted_iota(jnp.int32, shape, 1)
                column = lax.broadcasted_iota(jnp.int32, shape, 2)
                visible = [(column <= row).reshape(HEADS_AT_ONCE * rows, rows)]
            elif count == 2:
                visible = [my_y >= step, my_y >= NY - step]
            else:
                visible = [my_y >= step]
            for c, seen in enumerate(visible):
                c = c * blocks + q_block
                parts[c] = jnp.where(seen, parts[c], 0.0)
            here = pl.ds(first_head * rows, HEADS_AT_ONCE * rows)
            total = parts[0]
            for part in parts[1:]:
                total = total + part
            rounded = jnp.concatenate([part.astype(jnp.bfloat16) for part in parts], 1)
            given = jnp.dot(rounded, value_block, preferred_element_type=jnp.float32)
            if step is None:
                denoms[q_block, here] = total
                summed[q_block, here] = given
            else:
                denoms[q_block, here] += total
                summed[q_block, here] += given

    for copy in own[:2]:
        copy.wait()
    forward(0, 0)
    for dx in range(1, NX):
        from_head(dx, 0).wait_recv()
        from_head(dx, 1).wait_recv()
        forward(0, dx)
    for dx in range(1, NX):
        to_head(dx, 2).start()
    own[2].wait()
    for dx in range(1, NX):
        from_head(dx, 2).wait_recv()

    def arrive(step, i):
        ring(True, step, i).wait_recv()
        ring(False, step, i).wait_recv()
        forward(step, i)

    for i in range(NX):
        arrive(jnp.int32(1), i)
        attend(i, 0, 1, None)

    @pl.loop(2, 4)
    def _(step):
        for i in range(NX):
            arrive(step, i)
            attend(i, 2 * step - 3, 2, step - 1)

    for i in range(NX):
        attend(i, 5, 2, 3)
        ring(i < 2, jnp.int32(4), i).wait_recv()

    def give(block):
        dx = lax.rem(block - my_x + NX, NX)
        return pltpu.make_async_remote_copy(
            src_ref=finished.at[block],
            dst_ref=attended.at[my_x],
            send_sem=done_send.at[dx],
            recv_sem=done_recv.at[dx],
            device_id={"ctx": shifted(me, dx, 0)},
            device_id_type=MESH,
        )

    def take(dx):
        source = lax.rem(my_x - dx + NX, NX)
        return pltpu.make_async_remote_copy(
            src_ref=attended.at[source],
            dst_ref=attended.at[source],
            send_sem=done_send.at[dx],
            recv_sem=done_recv.at[dx],
            device_id={"ctx": shifted(me, dx, 0)},
            device_id_type=MESH,
        )

    for block in range(NX):
        attend(block, 7, 1, 4)
        denom = jnp.sum(denoms[block], -1, keepdims=True)
        finished[block] = (
            (summed[block] / denom).astype(jnp.bfloat16).reshape(GROUP, rows, HEAD_DIM)
        )

        @pl.when(my_x != block)
        def _():
            give(block).start()

    for small in smalls[1:]:
        small.wait()

    def stream_of(group, heads):
        columns = group_columns(group)
        attended_columns = jnp.concatenate([heads[h] for h in range(GROUP)], 1)
        stream = (
            tokens[:, columns].astype(jnp.float32) + attended_columns.astype(jnp.float32)
        ).astype(jnp.bfloat16)
        resid[:, columns] = stream
        packed = jnp.dot(held[...], stream, preferred_element_type=jnp.float32)
        return packed.astype(jnp.bfloat16).reshape(PEERS, SLOTS, group_width)

    def outward(k, part):
        return pltpu.make_async_remote_copy(
            src_ref=(first_out, rest_out)[part].at[k],
            dst_ref=(first_in, rest_in)[part].at[k],
            send_sem=out_send.at[part, k],
            recv_sem=out_recv.at[part, k],
            device_id={"ctx": to_peer(k)},
            device_id_type=MESH,
        )

    first_out[...] = stream_of(my_x, finished[my_x])

    @pl.loop(1, PEERS)
    def _(k):
        outward(k, 0).start()

    first_in[0] = first_out[0]

    for dx in range(1, NX):
        take(dx).wait_recv()
        source = lax.rem(my_x - dx + NX, NX)
        rest_out[:, dx - 1] = stream_of(source, attended[source])

    @pl.loop(1, PEERS)
    def _(k):
        outward(k, 1).start()

    rest_in[0] = rest_out[0]

    def norm(rows_in):
        wide = rows_in.astype(jnp.float32)
        mean_square = jnp.mean(wide * wide, -1, keepdims=True)
        wide_gain = gain[...].astype(jnp.float32).reshape(1, width)
        return (wide * lax.rsqrt(mean_square + epsilon) * wide_gain).astype(jnp.bfloat16)

    normed = norm(resid[...])

    def backward(k):
        return pltpu.make_async_remote_copy(
            src_ref=results.at[k],
            dst_ref=returns.at[k],
            send_sem=back_send.at[k],
            recv_sem=back_recv.at[k],
            device_id={"ctx": from_peer(k)},
            device_id_type=MESH,
        )

    logits = logit_cap * jnp.tanh(contract_last(router[...], normed) / logit_cap)
    plan = jnp.exp(logits)
    plan = plan / jnp.sum(plan, 0, keepdims=True)
    plans[0] = plan.astype(jnp.bfloat16)

    def plan_column(dy):
        return pltpu.make_async_remote_copy(
            src_ref=plans.at[0],
            dst_ref=plans.at[dy],
            send_sem=plan_send.at[dy],
            recv_sem=plan_recv.at[dy],
            device_id={"ctx": shifted(me, 0, dy)},
            device_id_type=MESH,
        )

    def plan_row(dx):
        return pltpu.make_async_remote_copy(
            src_ref=plans.at[pl.ds(0, NY)],
            dst_ref=plans.at[pl.ds(dx * NY, NY)],
            send_sem=plan_send.at[NY + dx],
            recv_sem=plan_recv.at[NY + dx],
            device_id={"ctx": shifted(me, dx, 0)},
            device_id_type=MESH,
        )

    for dy in range(1, NY):
        plan_column(dy).start()

    for load in loads:
        load.wait()

    @pl.loop(0, NX)
    def _(chunk):
        first = chunk * NY

        @pl.loop(jnp.maximum(first, 1), first + NY)
        def _(k):
            outward(k, 0).wait_recv()
            outward(k, 1).wait_recv()

        source = lax.rem(my_x - chunk + NX, NX)
        here = pl.ds(first, NY)
        landed[:, group_columns(source)] = first_in[here].reshape(NY * SLOTS, group_width)
        for dx in range(1, NX):
            landed[:, group_columns(lax.rem(source - dx + NX, NX))] = rest_in[
                here, dx - 1
            ].reshape(NY * SLOTS, group_width)
        block = norm(landed[...])
        gate = jnp.dot(block, gate_w[...], preferred_element_type=jnp.float32)
        upward = jnp.dot(block, up_w[...], preferred_element_type=jnp.float32)
        hidden = (gate / (1.0 + jnp.exp(-gate)) * upward).astype(jnp.bfloat16)
        given = jnp.dot(hidden, down_w[...], preferred_element_type=jnp.float32)
        results[pl.ds(first, NY)] = given.astype(jnp.bfloat16).reshape(NY, SLOTS, width)

        @pl.loop(jnp.maximum(first, 1), first + NY)
        def _(k):
            backward(k).start()

        @pl.when(chunk == 1)
        def _():
            for dy in range(1, NY):
                plan_column(dy).wait_recv()
            for dx in range(1, NX):
                plan_row(dx).start()

    returns[0] = results[0]

    for dx in range(1, NX):
        plan_row(dx).wait_recv()

    target = float(rows * PEERS * 2 / experts)

    def column_sums(scale):
        def add(s, total):
            block = plans[s].astype(jnp.float32)
            if scale is None:
                return total + block
            return total + block * (2.0 / jnp.sum(block * scale, 0, keepdims=True))

        total = lax.fori_loop(0, PEERS, add, jnp.zeros((experts, rows), jnp.float32), unroll=4)
        return jnp.sum(total, 1, keepdims=True)

    scale = target / column_sums(None)
    scale = lax.fori_loop(0, ITERS - 1, lambda _, s: target / column_sums(s), scale)
    plan = plan * scale
    plan = plan * (2.0 / jnp.sum(plan, 0, keepdims=True))
    named = lax.broadcasted_iota(jnp.int32, (experts, rows), 0)
    mass = [
        jnp.sum(jnp.where(named == picked[j : j + 1], plan, 0.0), 0, keepdims=True)
        for j in range(2)
    ]
    total = mass[0] + mass[1]
    gates = jnp.where(chosen[0], mass[0] / total, 0.0) + jnp.where(chosen[1], mass[1] / total, 0.0)
    mixing = jnp.where(place[:, None, :] == slot, gates[:, None, :], 0.0)
    mixing = mixing.reshape(PEERS * SLOTS, rows).T
    high = mixing.astype(jnp.bfloat16)
    low = (mixing - high.astype(jnp.float32)).astype(jnp.bfloat16)

    for part in range(3):
        for dx in range(1, NX):
            to_head(dx, part).wait_send()

    @pl.loop(1, 4)
    def _(step):
        @pl.loop(0, NX)
        def _(i):
            ring(True, step, i).wait_send()
            ring(False, step, i).wait_send()

    @pl.loop(0, 2)
    def _(i):
        ring(True, jnp.int32(4), i).wait_send()
        ring(False, jnp.int32(4), i + 2).wait_send()

    @pl.loop(1, NX)
    def _(dx):
        give(lax.rem(my_x + dx, NX)).wait_send()

    @pl.loop(1, PEERS)
    def _(k):
        outward(k, 0).wait_send()
        outward(k, 1).wait_send()

    for dy in range(1, NY):
        plan_column(dy).wait_send()
    for dx in range(1, NX):
        plan_row(dx).wait_send()

    def mix(k, first, last):
        columns = pl.ds(first, MIX_WIDTH)
        block = returns[k:last, :, columns].reshape((last - k) * SLOTS, MIX_WIDTH)
        here = slice(k * SLOTS, last * SLOTS)
        return jnp.dot(high[:, here], block, preferred_element_type=jnp.float32) + jnp.dot(
            low[:, here], block, preferred_element_type=jnp.float32
        )

    most = PEERS // 2

    @pl.loop(1, most)
    def _(k):
        backward(k).wait_recv()

    for first in range(0, width, MIX_WIDTH):
        columns = pl.ds(first, MIX_WIDTH)
        mixed[:, columns] = resid[:, columns].astype(jnp.float32) + mix(0, first, most)

    @pl.loop(most, PEERS)
    def _(k):
        backward(k).wait_recv()

    for first in range(0, width, MIX_WIDTH):
        columns = pl.ds(first, MIX_WIDTH)
        layer[:, columns] = (mixed[:, columns] + mix(most, first, PEERS)).astype(jnp.bfloat16)

    @pl.loop(1, PEERS)
    def _(k):
        backward(k).wait_send()


def per_device(tokens, queries, keys, values, norm_gain, router, w_gate, w_up, w_down, picks):
    rows, width = tokens.shape
    hidden = w_gate.shape[-1]
    experts = router.shape[1]
    whole = pl.BlockSpec(memory_space=pltpu.VMEM)
    apart = pl.BlockSpec(memory_space=pltpu.HBM)
    box = pltpu.VMEM((PEERS, SLOTS, width), jnp.bfloat16)
    sems = pltpu.SemaphoreType.DMA
    heads_of_block = pltpu.VMEM((NX, GROUP, rows, HEAD_DIM), jnp.bfloat16)
    running = pltpu.VMEM((NX, GROUP * rows, HEAD_DIM), jnp.float32)
    return pl.pallas_call(
        layer_kernel,
        out_shape=jax.ShapeDtypeStruct((rows, width), jnp.bfloat16),
        in_specs=[apart] * 10,
        out_specs=whole,
        scratch_shapes=[
            pltpu.VMEM((rows, width), jnp.bfloat16),
            pltpu.VMEM((width,), jnp.bfloat16),
            pltpu.VMEM((experts, width), jnp.bfloat16),
            pltpu.VMEM((2, rows), jnp.int32),
            pltpu.VMEM((width, hidden), jnp.bfloat16),
            pltpu.VMEM((width, hidden), jnp.bfloat16),
            pltpu.VMEM((hidden, width), jnp.bfloat16),
            pltpu.VMEM((NX, rows, GROUP * HEAD_DIM), jnp.bfloat16),
            pltpu.VMEM((NY, NX, 2, rows, HEAD_DIM), jnp.bfloat16),
            running,
            running,
            heads_of_block,
            heads_of_block,
            pltpu.VMEM((rows, width), jnp.bfloat16),
            pltpu.VMEM((PEERS * SLOTS, rows), jnp.bfloat16),
            pltpu.VMEM((rows, width), jnp.float32),
            pltpu.VMEM((PEERS, SLOTS, GROUP * HEAD_DIM), jnp.bfloat16),
            pltpu.VMEM((PEERS, NX - 1, SLOTS, GROUP * HEAD_DIM), jnp.bfloat16),
            pltpu.VMEM((PEERS, SLOTS, GROUP * HEAD_DIM), jnp.bfloat16),
            pltpu.VMEM((PEERS, NX - 1, SLOTS, GROUP * HEAD_DIM), jnp.bfloat16),
            pltpu.VMEM((NY * SLOTS, width), jnp.bfloat16),
            box,
            box,
            pltpu.VMEM((PEERS, experts, rows), jnp.bfloat16),
            sems((4,)),
            sems((3,)),
            sems((3,)),
            sems((NX, 3)),
            sems((NX, 3)),
            sems((2, 5, NX)),
            sems((2, 5, NX)),
            sems((NX,)),
            sems((NX,)),
            sems((NY + NX,)),
            sems((NY + NX,)),
            sems((2, PEERS)),
            sems((2, PEERS)),
            sems((PEERS,)),
            sems((PEERS,)),
        ],
        compiler_params=pltpu.CompilerParams(
            collective_id=1, has_side_effects=True, vmem_limit_bytes=VMEM_LIMIT
        ),
        name="layer",
    )(
        tokens,
        norm_gain,
        router.T,
        picks.T,
        queries,
        keys,
        values,
        w_gate[0],
        w_up[0],
        w_down[0],
    )


def solution(mesh):
    placed = (
        P(("seq", "ctx"), None),
        P(("seq", "ctx"), None),
        P(("seq", "ctx"), None),
        P(("seq", "ctx"), None),
        P(),
        P(),
        P("ctx", None, None),
        P("ctx", None, None),
        P("ctx", None, None),
        P(("seq", "ctx"), None),
    )
    return jax.shard_map(
        per_device, mesh=mesh, in_specs=placed, out_specs=P(("seq", "ctx"), None), check_vma=False
    )
```

```python
import math

import jax
import jax.numpy as jnp
from jax import lax
from jax.experimental import pallas as pl
from jax.experimental.pallas import tpu as pltpu
from jax.sharding import PartitionSpec as P

HEADS = 16
KV_HEADS = 4
GROUP = HEADS // KV_HEADS
HEAD_DIM = 128
ITERS = 8
MESH = pl.DeviceIdType.MESH
NX = 4
NY = 8
PEERS = NX * NY
SLOTS = 8
MIX_WIDTH = 512
HEADS_AT_ONCE = 4
VMEM_LIMIT = 60 * 1024 * 1024


score_cap = 50.0
logit_cap = 10.0
epsilon = 1e-06


def shifted(me, dx, dy):
    return lax.rem(me // NY + dx + NX, NX) * NY + lax.rem(lax.rem(me, NY) + dy + NY, NY)


def contract_last(left, right):
    return lax.dot_general(
        left, right, (((1,), (1,)), ((), ())), preferred_element_type=jnp.float32
    )


def layer_kernel(
    tokens_in,
    gain_in,
    router_in,
    picks_in,
    queries,
    keys,
    values,
    w_gate,
    w_up,
    w_down,
    layer,
    tokens,
    gain,
    router,
    picks,
    gate_w,
    up_w,
    down_w,
    query_rows,
    pairs,
    summed,
    denoms,
    finished,
    attended,
    resid,
    held,
    mixed,
    first_out,
    rest_out,
    first_in,
    rest_in,
    landed,
    results,
    returns,
    plans,
    small_sem,
    weight_sem,
    own_sem,
    head_send,
    head_recv,
    ring_send,
    ring_recv,
    done_send,
    done_recv,
    plan_send,
    plan_recv,
    out_send,
    out_recv,
    back_send,
    back_recv,
):
    me = lax.axis_index("ctx")
    my_x = me // NY
    my_y = lax.rem(me, NY)
    rows, width = tokens.shape
    experts = router.shape[0]
    group_width = GROUP * HEAD_DIM

    def to_peer(k):
        return shifted(me, k // NY, lax.rem(k, NY))

    def from_peer(k):
        return shifted(me, -(k // NY), -lax.rem(k, NY))

    barrier = pltpu.get_barrier_semaphore()

    near = [shifted(me, dx, 0) for dx in range(1, NX)] + [shifted(me, 0, dy) for dy in (1, -1)]
    for peer in near:
        pl.semaphore_signal(barrier, inc=1, device_id={"ctx": peer}, device_id_type=MESH)

    smalls = [
        pltpu.make_async_copy(src, dst, small_sem.at[i])
        for i, (src, dst) in enumerate(
            ((picks_in, picks), (tokens_in, tokens), (gain_in, gain), (router_in, router))
        )
    ]
    smalls[0].start()

    def head_columns(head):
        return pl.ds(pl.multiple_of(head * HEAD_DIM, HEAD_DIM), HEAD_DIM)

    def group_columns(head):
        return pl.ds(pl.multiple_of(head * group_width, group_width), group_width)

    own = [
        (keys.at[:, head_columns(my_x)], pairs.at[0, my_x, 0]),
        (values.at[:, head_columns(my_x)], pairs.at[0, my_x, 1]),
        (queries.at[:, group_columns(my_x)], query_rows.at[my_x]),
    ]
    own = [pltpu.make_async_copy(src, dst, own_sem.at[i]) for i, (src, dst) in enumerate(own)]
    for copy in own:
        copy.start()
    loads = [
        pltpu.make_async_copy(src, dst, weight_sem.at[i])
        for i, (src, dst) in enumerate(((w_gate, gate_w), (w_up, up_w), (w_down, down_w)))
    ]

    def to_head(dx, part):
        head = lax.rem(my_x + dx, NX)
        if part == 2:
            src, dst = queries.at[:, group_columns(head)], query_rows.at[my_x]
        else:
            src = (keys, values)[part].at[:, head_columns(head)]
            dst = pairs.at[0, my_x, part]
        return pltpu.make_async_remote_copy(
            src_ref=src,
            dst_ref=dst,
            send_sem=head_send.at[dx, part],
            recv_sem=head_recv.at[dx, part],
            device_id={"ctx": shifted(me, dx, 0)},
            device_id_type=MESH,
        )

    def from_head(dx, part):
        source = lax.rem(my_x - dx + NX, NX)
        dst = query_rows.at[source] if part == 2 else pairs.at[0, source, part]
        return pltpu.make_async_remote_copy(
            src_ref=dst,
            dst_ref=dst,
            send_sem=head_send.at[dx, part],
            recv_sem=head_recv.at[dx, part],
            device_id={"ctx": shifted(me, dx, 0)},
            device_id_type=MESH,
        )

    pl.semaphore_wait(barrier, len(near))
    for dx in range(1, NX):
        for part in range(2):
            to_head(dx, part).start()

    smalls[0].wait()
    picked = picks[...]
    offset = lax.rem(picked // NY - my_x + NX, NX) * NY + lax.rem(
        lax.rem(picked, NY) - my_y + NY, NY
    )
    number = lax.broadcasted_iota(jnp.int32, (PEERS, rows), 0)
    chosen = [number == offset[j : j + 1] for j in range(2)]
    either = jnp.where(chosen[0] | chosen[1], 1.0, 0.0)
    earlier = jnp.where(
        lax.broadcasted_iota(jnp.int32, (rows, rows), 0)
        < lax.broadcasted_iota(jnp.int32, (rows, rows), 1),
        1.0,
        0.0,
    ).astype(jnp.bfloat16)
    ranks = jnp.dot(either.astype(jnp.bfloat16), earlier, preferred_element_type=jnp.float32)
    place = jnp.where(either > 0.0, ranks, -1.0)
    slot = lax.broadcasted_iota(jnp.int32, (PEERS, SLOTS, rows), 1).astype(jnp.float32)
    rows_held = jnp.where(place[:, None, :] == slot, 1.0, 0.0).reshape(PEERS * SLOTS, rows)
    held[...] = rows_held.astype(jnp.bfloat16)

    def behind(step):
        return lax.select(step == 0, 0, 2 * step - 1)

    def ahead(step):
        return lax.select(step == 4, 7, 2 * step)

    def ring(up, step, i):
        block = lax.rem(my_x - i + NX, NX)
        place_of = behind if up else ahead
        way = 0 if up else 1
        return pltpu.make_async_remote_copy(
            src_ref=pairs.at[place_of(step - 1), block],
            dst_ref=pairs.at[place_of(step), block],
            send_sem=ring_send.at[way, step, i],
            recv_sem=ring_recv.at[way, step, i],
            device_id={"ctx": shifted(me, 0, 1 if up else -1)},
            device_id_type=MESH,
        )

    def forward(step, i):
        step = jnp.int32(step)

        @pl.when((step < 3) | (i < 2))
        def _():
            ring(True, step + 1, i).start()

        @pl.when((step < 3) | (i >= 2))
        def _():
            ring(False, step + 1, i).start()

    def attend(q_block, first, count, step):
        blocks = q_block + 1
        units = pairs[pl.ds(first, count), :blocks]
        key_block = units[:, :, 0].reshape(count * blocks * rows, HEAD_DIM)
        value_block = units[:, :, 1].reshape(count * blocks * rows, HEAD_DIM)
        for first_head in range(0, GROUP, HEADS_AT_ONCE):
            heads = range(first_head, first_head + HEADS_AT_ONCE)
            query = [query_rows[q_block, :, h * HEAD_DIM : (h + 1) * HEAD_DIM] for h in heads]
            query = jnp.concatenate(query, 0)
            scores = contract_last(query, key_block)
            weights = jnp.exp2(
                jnp.tanh(scores * (1.0 / (score_cap * math.sqrt(HEAD_DIM))))
                * (score_cap * math.log2(math.e))
            )
            parts = [weights[:, c : c + rows] for c in range(0, weights.shape[1], rows)]
            if step is None:
                shape = (HEADS_AT_ONCE, rows, rows)
                row = lax.broadcasted_iota(jnp.int32, shape, 1)
                column = lax.broadcasted_iota(jnp.int32, shape, 2)
                visible = [(column <= row).reshape(HEADS_AT_ONCE * rows, rows)]
            elif count == 2:
                visible = [my_y >= step, my_y >= NY - step]
            else:
                visible = [my_y >= step]
            for c, seen in enumerate(visible):
                c = c * blocks + q_block
                parts[c] = jnp.where(seen, parts[c], 0.0)
            here = pl.ds(first_head * rows, HEADS_AT_ONCE * rows)
            total = parts[0]
            for part in parts[1:]:
                total = total + part
            rounded = jnp.concatenate([part.astype(jnp.bfloat16) for part in parts], 1)
            given = jnp.dot(rounded, value_block, preferred_element_type=jnp.float32)
            if step is None:
                denoms[q_block, here] = total
                summed[q_block, here] = given
            else:
                denoms[q_block, here] += total
                summed[q_block, here] += given

    for copy in own[:2]:
        copy.wait()
    forward(0, 0)
    for dx in range(1, NX):
        from_head(dx, 0).wait_recv()
        from_head(dx, 1).wait_recv()
        forward(0, dx)
    for dx in range(1, NX):
        to_head(dx, 2).start()
    for load in smalls[1:] + loads:
        load.start()
    own[2].wait()
    for dx in range(1, NX):
        from_head(dx, 2).wait_recv()

    def arrive(step, i):
        ring(True, step, i).wait_recv()
        ring(False, step, i).wait_recv()
        forward(step, i)

    for i in range(NX):
        arrive(jnp.int32(1), i)
        attend(i, 0, 1, None)

    @pl.loop(2, 4)
    def _(step):
        for i in range(NX):
            arrive(step, i)
            attend(i, 2 * step - 3, 2, step - 1)

    for i in range(NX):
        attend(i, 5, 2, 3)
        ring(i < 2, jnp.int32(4), i).wait_recv()

    def give(block):
        dx = lax.rem(block - my_x + NX, NX)
        return pltpu.make_async_remote_copy(
            src_ref=finished.at[block],
            dst_ref=attended.at[my_x],
            send_sem=done_send.at[dx],
            recv_sem=done_recv.at[dx],
            device_id={"ctx": shifted(me, dx, 0)},
            device_id_type=MESH,
        )

    def take(dx):
        source = lax.rem(my_x - dx + NX, NX)
        return pltpu.make_async_remote_copy(
            src_ref=attended.at[source],
            dst_ref=attended.at[source],
            send_sem=done_send.at[dx],
            recv_sem=done_recv.at[dx],
            device_id={"ctx": shifted(me, dx, 0)},
            device_id_type=MESH,
        )

    for block in range(NX):
        attend(block, 7, 1, 4)
        denom = jnp.sum(denoms[block], -1, keepdims=True)
        finished[block] = (
            (summed[block] / denom).astype(jnp.bfloat16).reshape(GROUP, rows, HEAD_DIM)
        )

        @pl.when(my_x != block)
        def _():
            give(block).start()

    for small in smalls[1:]:
        small.wait()

    def stream_of(group, heads):
        columns = group_columns(group)
        attended_columns = jnp.concatenate([heads[h] for h in range(GROUP)], 1)
        stream = (
            tokens[:, columns].astype(jnp.float32) + attended_columns.astype(jnp.float32)
        ).astype(jnp.bfloat16)
        resid[:, columns] = stream
        packed = jnp.dot(held[...], stream, preferred_element_type=jnp.float32)
        return packed.astype(jnp.bfloat16).reshape(PEERS, SLOTS, group_width)

    def outward(k, part):
        return pltpu.make_async_remote_copy(
            src_ref=(first_out, rest_out)[part].at[k],
            dst_ref=(first_in, rest_in)[part].at[k],
            send_sem=out_send.at[part, k],
            recv_sem=out_recv.at[part, k],
            device_id={"ctx": to_peer(k)},
            device_id_type=MESH,
        )

    first_out[...] = stream_of(my_x, finished[my_x])

    @pl.loop(1, PEERS)
    def _(k):
        outward(k, 0).start()

    first_in[0] = first_out[0]

    for dx in range(1, NX):
        take(dx).wait_recv()
        source = lax.rem(my_x - dx + NX, NX)
        rest_out[:, dx - 1] = stream_of(source, attended[source])

    @pl.loop(1, PEERS)
    def _(k):
        outward(k, 1).start()

    rest_in[0] = rest_out[0]

    def norm(rows_in):
        wide = rows_in.astype(jnp.float32)
        mean_square = jnp.mean(wide * wide, -1, keepdims=True)
        wide_gain = gain[...].astype(jnp.float32).reshape(1, width)
        return (wide * lax.rsqrt(mean_square + epsilon) * wide_gain).astype(jnp.bfloat16)

    normed = norm(resid[...])

    def backward(k):
        return pltpu.make_async_remote_copy(
            src_ref=results.at[k],
            dst_ref=returns.at[k],
            send_sem=back_send.at[k],
            recv_sem=back_recv.at[k],
            device_id={"ctx": from_peer(k)},
            device_id_type=MESH,
        )

    logits = logit_cap * jnp.tanh(contract_last(router[...], normed) / logit_cap)
    plan = jnp.exp(logits)
    plan = plan / jnp.sum(plan, 0, keepdims=True)
    plans[0] = plan.astype(jnp.bfloat16)

    def plan_column(dy):
        return pltpu.make_async_remote_copy(
            src_ref=plans.at[0],
            dst_ref=plans.at[dy],
            send_sem=plan_send.at[dy],
            recv_sem=plan_recv.at[dy],
            device_id={"ctx": shifted(me, 0, dy)},
            device_id_type=MESH,
        )

    def plan_row(dx):
        return pltpu.make_async_remote_copy(
            src_ref=plans.at[pl.ds(0, NY)],
            dst_ref=plans.at[pl.ds(dx * NY, NY)],
            send_sem=plan_send.at[NY + dx],
            recv_sem=plan_recv.at[NY + dx],
            device_id={"ctx": shifted(me, dx, 0)},
            device_id_type=MESH,
        )

    for dy in range(1, NY):
        plan_column(dy).start()

    for load in loads:
        load.wait()

    @pl.loop(0, NX)
    def _(chunk):
        first = chunk * NY

        @pl.loop(jnp.maximum(first, 1), first + NY)
        def _(k):
            outward(k, 0).wait_recv()
            outward(k, 1).wait_recv()

        source = lax.rem(my_x - chunk + NX, NX)
        here = pl.ds(first, NY)
        landed[:, group_columns(source)] = first_in[here].reshape(NY * SLOTS, group_width)
        for dx in range(1, NX):
            landed[:, group_columns(lax.rem(source - dx + NX, NX))] = rest_in[
                here, dx - 1
            ].reshape(NY * SLOTS, group_width)
        block = norm(landed[...])
        gate = jnp.dot(block, gate_w[...], preferred_element_type=jnp.float32)
        upward = jnp.dot(block, up_w[...], preferred_element_type=jnp.float32)
        hidden = (gate / (1.0 + jnp.exp(-gate)) * upward).astype(jnp.bfloat16)
        given = jnp.dot(hidden, down_w[...], preferred_element_type=jnp.float32)
        results[pl.ds(first, NY)] = given.astype(jnp.bfloat16).reshape(NY, SLOTS, width)

        @pl.loop(jnp.maximum(first, 1), first + NY)
        def _(k):
            backward(k).start()

        @pl.when(chunk == 1)
        def _():
            for dy in range(1, NY):
                plan_column(dy).wait_recv()
            for dx in range(1, NX):
                plan_row(dx).start()

    returns[0] = results[0]

    for dx in range(1, NX):
        plan_row(dx).wait_recv()

    target = float(rows * PEERS * 2 / experts)

    def column_sums(scale):
        def add(s, total):
            block = plans[s].astype(jnp.float32)
            if scale is None:
                return total + block
            return total + block * (2.0 / jnp.sum(block * scale, 0, keepdims=True))

        total = lax.fori_loop(0, PEERS, add, jnp.zeros((experts, rows), jnp.float32), unroll=4)
        return jnp.sum(total, 1, keepdims=True)

    scale = target / column_sums(None)
    scale = lax.fori_loop(0, ITERS - 1, lambda _, s: target / column_sums(s), scale)
    plan = plan * scale
    plan = plan * (2.0 / jnp.sum(plan, 0, keepdims=True))
    named = lax.broadcasted_iota(jnp.int32, (experts, rows), 0)
    mass = [
        jnp.sum(jnp.where(named == picked[j : j + 1], plan, 0.0), 0, keepdims=True)
        for j in range(2)
    ]
    total = mass[0] + mass[1]
    gates = jnp.where(chosen[0], mass[0] / total, 0.0) + jnp.where(chosen[1], mass[1] / total, 0.0)
    mixing = jnp.where(place[:, None, :] == slot, gates[:, None, :], 0.0)
    mixing = mixing.reshape(PEERS * SLOTS, rows).T
    high = mixing.astype(jnp.bfloat16)
    low = (mixing - high.astype(jnp.float32)).astype(jnp.bfloat16)

    for part in range(3):
        for dx in range(1, NX):
            to_head(dx, part).wait_send()

    @pl.loop(1, 4)
    def _(step):
        @pl.loop(0, NX)
        def _(i):
            ring(True, step, i).wait_send()
            ring(False, step, i).wait_send()

    @pl.loop(0, 2)
    def _(i):
        ring(True, jnp.int32(4), i).wait_send()
        ring(False, jnp.int32(4), i + 2).wait_send()

    @pl.loop(1, NX)
    def _(dx):
        give(lax.rem(my_x + dx, NX)).wait_send()

    @pl.loop(1, PEERS)
    def _(k):
        outward(k, 0).wait_send()
        outward(k, 1).wait_send()

    for dy in range(1, NY):
        plan_column(dy).wait_send()
    for dx in range(1, NX):
        plan_row(dx).wait_send()

    def mix(k, first, last):
        columns = pl.ds(first, MIX_WIDTH)
        block = returns[k:last, :, columns].reshape((last - k) * SLOTS, MIX_WIDTH)
        here = slice(k * SLOTS, last * SLOTS)
        return jnp.dot(high[:, here], block, preferred_element_type=jnp.float32) + jnp.dot(
            low[:, here], block, preferred_element_type=jnp.float32
        )

    most = PEERS // 2

    @pl.loop(1, most)
    def _(k):
        backward(k).wait_recv()

    for first in range(0, width, MIX_WIDTH):
        columns = pl.ds(first, MIX_WIDTH)
        mixed[:, columns] = resid[:, columns].astype(jnp.float32) + mix(0, first, most)

    @pl.loop(most, PEERS)
    def _(k):
        backward(k).wait_recv()

    for first in range(0, width, MIX_WIDTH):
        columns = pl.ds(first, MIX_WIDTH)
        layer[:, columns] = (mixed[:, columns] + mix(most, first, PEERS)).astype(jnp.bfloat16)

    @pl.loop(1, PEERS)
    def _(k):
        backward(k).wait_send()


def per_device(tokens, queries, keys, values, norm_gain, router, w_gate, w_up, w_down, picks):
    rows, width = tokens.shape
    hidden = w_gate.shape[-1]
    experts = router.shape[1]
    whole = pl.BlockSpec(memory_space=pltpu.VMEM)
    apart = pl.BlockSpec(memory_space=pltpu.HBM)
    box = pltpu.VMEM((PEERS, SLOTS, width), jnp.bfloat16)
    sems = pltpu.SemaphoreType.DMA
    heads_of_block = pltpu.VMEM((NX, GROUP, rows, HEAD_DIM), jnp.bfloat16)
    running = pltpu.VMEM((NX, GROUP * rows, HEAD_DIM), jnp.float32)
    return pl.pallas_call(
        layer_kernel,
        out_shape=jax.ShapeDtypeStruct((rows, width), jnp.bfloat16),
        in_specs=[apart] * 10,
        out_specs=whole,
        scratch_shapes=[
            pltpu.VMEM((rows, width), jnp.bfloat16),
            pltpu.VMEM((width,), jnp.bfloat16),
            pltpu.VMEM((experts, width), jnp.bfloat16),
            pltpu.VMEM((2, rows), jnp.int32),
            pltpu.VMEM((width, hidden), jnp.bfloat16),
            pltpu.VMEM((width, hidden), jnp.bfloat16),
            pltpu.VMEM((hidden, width), jnp.bfloat16),
            pltpu.VMEM((NX, rows, GROUP * HEAD_DIM), jnp.bfloat16),
            pltpu.VMEM((NY, NX, 2, rows, HEAD_DIM), jnp.bfloat16),
            running,
            running,
            heads_of_block,
            heads_of_block,
            pltpu.VMEM((rows, width), jnp.bfloat16),
            pltpu.VMEM((PEERS * SLOTS, rows), jnp.bfloat16),
            pltpu.VMEM((rows, width), jnp.float32),
            pltpu.VMEM((PEERS, SLOTS, GROUP * HEAD_DIM), jnp.bfloat16),
            pltpu.VMEM((PEERS, NX - 1, SLOTS, GROUP * HEAD_DIM), jnp.bfloat16),
            pltpu.VMEM((PEERS, SLOTS, GROUP * HEAD_DIM), jnp.bfloat16),
            pltpu.VMEM((PEERS, NX - 1, SLOTS, GROUP * HEAD_DIM), jnp.bfloat16),
            pltpu.VMEM((NY * SLOTS, width), jnp.bfloat16),
            box,
            box,
            pltpu.VMEM((PEERS, experts, rows), jnp.bfloat16),
            sems((4,)),
            sems((3,)),
            sems((3,)),
            sems((NX, 3)),
            sems((NX, 3)),
            sems((2, 5, NX)),
            sems((2, 5, NX)),
            sems((NX,)),
            sems((NX,)),
            sems((NY + NX,)),
            sems((NY + NX,)),
            sems((2, PEERS)),
            sems((2, PEERS)),
            sems((PEERS,)),
            sems((PEERS,)),
        ],
        compiler_params=pltpu.CompilerParams(
            collective_id=1, has_side_effects=True, vmem_limit_bytes=VMEM_LIMIT
        ),
        name="layer",
    )(
        tokens,
        norm_gain,
        router.T,
        picks.T,
        queries,
        keys,
        values,
        w_gate[0],
        w_up[0],
        w_down[0],
    )


def solution(mesh):
    placed = (
        P(("seq", "ctx"), None),
        P(("seq", "ctx"), None),
        P(("seq", "ctx"), None),
        P(("seq", "ctx"), None),
        P(),
        P(),
        P("ctx", None, None),
        P("ctx", None, None),
        P("ctx", None, None),
        P(("seq", "ctx"), None),
    )
    return jax.shard_map(
        per_device, mesh=mesh, in_specs=placed, out_specs=P(("seq", "ctx"), None), check_vma=False
    )
```
